32 devices in a mesh: bulk: 16 (over z, x, core), span: 2 (over y).
Axes of the slice: x: 2, y: 2, z: 4, core: 2. Of those that a mesh axis runs over, the one named last changes fastest.
Arguments:
- snapshots: float32 [65536, 128], P(('span', 'bulk'))
- jac_blocks: bfloat16 [512, 4, 128, 128], P(('span', 'bulk'))
- jac_cols: int32 [512, 4], P(('span', 'bulk')), may hold values from 0 to 511, as said below
Outputs:
- modes: float32 [65536, 128], P(('span', 'bulk'))
- factor: float32 [128, 128], replicated
- jac_modes: bfloat16 [65536, 128], P(('span', 'bulk'))
- reduced: float32 [128, 128], replicated
The draws below stay inside these ranges and needn't reach their ends.
Inputs may be any that keep to these rules, and one draw needn't show every extreme that they name: jac_cols[r, 0] = r. Every column block lies in the die region of r (aligned runs of 256 block rows) and within 16 block rows of the shard of 16 block rows that holds r.
All inputs are finite; a program needn't handle non-finite values.
Results may differ from the reference program's by a relative error of at most 0.0029.
The reference program's roundings to bfloat16 on the way (of `modes_b`) count: a program that leaves them out, or rounds other values in their place, can miss the bound.
Values may be sent and summed in bfloat16 or wider, within the bound.
No kernel may reach another device: no remote copies, remote signals or barrier semaphores. Data moves between devices by JAX's collectives and lax.ppermute only.
A program may use at most 64 MiB of HBM per device.

```python
import math
import jax
import jax.numpy as jnp
from jax import lax

K = 128
BLOCK = 128
NB = 4
RB_DEV = 16
REGION = 256
ROWBLOCKS = 512
ROWS = 65536


def draw_snapshots(key, part):
    key_base = jax.random.fold_in(key, 0)
    key_order = jax.random.fold_in(key, 3)
    key_cols = jax.random.fold_in(key, 4)
    key_sign = jax.random.fold_in(key, 5)
    index = jnp.arange(K, dtype=jnp.float32)
    singular = 3.0 * jnp.exp(-math.log(2500.0) * index / (K - 1))
    order = jax.random.permutation(key_order, K)
    singular = jnp.take(singular, order)
    table = jnp.cos(math.pi * (index[:, None] + 0.5) * index[None, :] / K) * math.sqrt(2.0 / K)
    table = table * jnp.where(index == 0.0, math.sqrt(0.5), 1.0)[None, :]
    mixing = singular[:, None] * table.T
    columns = jax.random.permutation(key_cols, K)
    signs = (2 * jax.random.randint(key_sign, (K,), 0, 2, dtype=jnp.int32) - 1).astype(jnp.float32)
    mixing = jnp.take(mixing, columns, axis=1) * signs[None, :]
    base = jax.random.normal(key_base, (ROWS, K), jnp.float32)
    return jnp.dot(base, mixing, precision=lax.Precision.HIGHEST, preferred_element_type=jnp.float32)


def draw_jac_cols(key, part):
    block_ids = jnp.arange(ROWBLOCKS, dtype=jnp.int32)
    region_low = block_ids // REGION * REGION
    region_high = region_low + REGION - 1
    shard_start = block_ids // RB_DEV * RB_DEV
    offsets = jax.random.randint(key, (ROWBLOCKS, NB - 1), -RB_DEV, 2 * RB_DEV, dtype=jnp.int32)
    others = jnp.clip(shard_start[:, None] + offsets, region_low[:, None], region_high[:, None])
    return jnp.concatenate([block_ids[:, None], others], axis=1).astype(jnp.int32)


def draw_jac_blocks(key, part):
    key_val, key_diag = jax.random.split(key, 2)
    shape = (ROWBLOCKS, NB, BLOCK, BLOCK)
    values = jax.random.normal(key_val, shape, jnp.float32)
    values = values * (1.5 / math.sqrt(BLOCK * NB))
    rising = 1.0 + 2.0 * jnp.arange(ROWBLOCKS, dtype=jnp.float32) / ROWBLOCKS
    spread = jnp.exp(jax.random.uniform(key_diag, (ROWBLOCKS, BLOCK), jnp.float32, 0.0, math.log(3.0)))
    diag_vals = rising[:, None] * spread
    identity = jnp.eye(BLOCK, dtype=jnp.float32)
    first_slot = (jnp.arange(NB) == 0).astype(jnp.float32)
    extra = diag_vals[:, None, :, None] * identity[None, None, :, :] * first_slot[None, :, None, None]
    return (values + extra).astype(jnp.bfloat16)


def setup_inputs(seed: int = 0) -> dict:
    arg_keys = jax.random.split(jax.random.key(seed), 4)
    return {
        "snapshots": draw_snapshots(jax.random.fold_in(arg_keys[3], 71), 0),
        "jac_blocks": draw_jac_blocks(jax.random.fold_in(arg_keys[3], 71), 0),
        "jac_cols": draw_jac_cols(jax.random.fold_in(arg_keys[3], 71), 0),
    }


def cholesky_step(data):
    high = lax.Precision.HIGHEST
    gram = lax.dot_general(data.astype(jnp.float32), data.astype(jnp.float32), (((0,), (0,)), ((), ())), precision=high, preferred_element_type=jnp.float32) / ROWS
    lower = jnp.linalg.cholesky(gram)
    inverse = lax.linalg.triangular_solve(lower, jnp.eye(K, dtype=jnp.float32), left_side=True, lower=True)
    result = jnp.dot(data.astype(jnp.float32), inverse.T.astype(jnp.float32), precision=high, preferred_element_type=jnp.float32)
    return (result, lower)

def reference(snapshots, jac_blocks, jac_cols):
    high = lax.Precision.HIGHEST
    first, lower1 = cholesky_step(snapshots)
    modes, lower2 = cholesky_step(first)
    factor = jnp.dot(lower2.T.astype(jnp.float32), lower1.T.astype(jnp.float32), precision=high, preferred_element_type=jnp.float32)
    modes_b = modes.astype(jnp.bfloat16)
    mode_blocks = modes_b.reshape(ROWBLOCKS, BLOCK, K)
    groups = ROWBLOCKS // RB_DEV
    blocks_grouped = jac_blocks.reshape(groups, RB_DEV, NB, BLOCK, BLOCK)
    cols_grouped = jac_cols.reshape(groups, RB_DEV, NB)

    def one_group(pair):
        blocks, cols = pair
        picked = jnp.take(mode_blocks, cols.astype(jnp.int32), axis=0)
        product = jnp.einsum('rnij,rnjk->rik', blocks.astype(jnp.float32), picked.astype(jnp.float32), precision=high)
        return product.astype(jnp.bfloat16).reshape(RB_DEV * BLOCK, K)
    jac_modes = lax.map(one_group, (blocks_grouped, cols_grouped)).reshape(ROWS, K)
    reduced = lax.dot_general(modes.astype(jnp.float32), jac_modes.astype(jnp.float32), (((0,), (0,)), ((), ())), precision=high, preferred_element_type=jnp.float32) / ROWS
    return (modes, factor, jac_modes, reduced)
```

```python
import jax
import jax.numpy as jnp
from jax import lax
from jax.experimental import pallas as pl
from jax.experimental.pallas import tpu as pltpu
from jax.sharding import PartitionSpec as P

F32 = jnp.float32
BF16 = jnp.bfloat16
HIGH = lax.Precision.HIGHEST
VMEM_LIMIT = 48 * 1024 * 1024


def mm(a, b):
    return lax.dot_general(a, b, (((1,), (0,)), ((), ())), preferred_element_type=F32)


def mm_tn(a, b):
    return lax.dot_general(a, b, (((0,), (0,)), ((), ())), preferred_element_type=F32)


def split2(x):
    h = x.astype(BF16)
    return h, (x - h.astype(F32)).astype(BF16)


def split3(x):
    h = x.astype(BF16)
    r = x - h.astype(F32)
    m = r.astype(BF16)
    return h, m, (r - m.astype(F32)).astype(BF16)


def rows_of(i, n):
    return pl.ds(pl.multiple_of(i * n, n), n)


def gram_kernel(s_ref, g_ref):
    rows, k = s_ref.shape
    step = 256
    hh = jnp.zeros((2 * k, 2 * k), F32)
    hl = jnp.zeros((k, k), F32)
    for c in range(rows // step):
        h, m, l = split3(s_ref[c * step : (c + 1) * step, :])
        hm = jnp.concatenate([h, m], axis=1)
        hh = hh + mm_tn(hm, hm)
        hl = hl + mm_tn(h, l)
    cross = hh[:k, k:] + hl
    g_ref[...] = hh[:k, :k] + (cross + cross.T + hh[k:, k:])


def local_gram(s):
    k = s.shape[1]
    return pl.pallas_call(
        gram_kernel,
        out_shape=jax.ShapeDtypeStruct((k, k), F32),
        compiler_params=pltpu.CompilerParams(vmem_limit_bytes=VMEM_LIMIT),
        name="local_gram",
    )(s)


def rsqrt_newton(d):
    y = lax.rsqrt(d)
    return y * (1.5 - (0.5 * d) * (y * y))


def factor_and_inverse(a):
    k = a.shape[0]
    blocks = [a[8 * i : 8 * i + 8, :] for i in range(k // 8)]
    lane = lax.broadcasted_iota(jnp.int32, (8, k), 1)
    sub = lax.broadcasted_iota(jnp.int32, (8, k), 0)
    for j in range(k):
        b, s = divmod(j, 8)
        row = jnp.broadcast_to(blocks[b][s : s + 1, :], (8, k))
        d = jnp.broadcast_to(row[:, j : j + 1], (8, k))
        rs = rsqrt_newton(d)
        u = row * rs
        here = lane == j
        v = jnp.where(here, rs, u)
        for i in range(b, k // 8):
            x = blocks[i]
            c = jnp.broadcast_to(x[:, j : j + 1], (8, k)) * rs
            new = jnp.where(here, 0.0, x) - c * v
            if i == b:
                new = jnp.where(sub > s, new, jnp.where(sub == s, u, x))
            blocks[i] = new
    x = jnp.concatenate(blocks, axis=0)
    r = lax.broadcasted_iota(jnp.int32, (k, k), 0)
    c = lax.broadcasted_iota(jnp.int32, (k, k), 1)
    upper = jnp.where(c >= r, x, 0.0)
    inverse = jnp.where(c < r, x, jnp.where(c == r, 1.0 / x, 0.0))
    return upper, inverse


def chol1_kernel(rows_total, g_ref, up_ref, w1_ref, w2_ref):
    k = g_ref.shape[0]
    g = g_ref[...] / rows_total
    up, inv = factor_and_inverse(0.5 * (g + g.T))
    up_ref[...] = up
    h, m, l = split3(inv.T)
    hm = jnp.concatenate([h, m], axis=1)
    w1_ref[...] = jnp.concatenate([hm, hm], axis=0)
    w2_ref[...] = jnp.concatenate([l, h], axis=0)


def chol1(g, rows_total):
    k = g.shape[0]
    return pl.pallas_call(
        lambda *refs: chol1_kernel(rows_total, *refs),
        out_shape=(
            jax.ShapeDtypeStruct((k, k), F32),
            jax.ShapeDtypeStruct((2 * k, 2 * k), BF16),
            jax.ShapeDtypeStruct((2 * k, k), BF16),
        ),
        compiler_params=pltpu.CompilerParams(vmem_limit_bytes=VMEM_LIMIT),
        name="factor_first",
    )(g)


def chol2_kernel(rows_total, g_ref, t_ref, up1_ref, w1_ref, fac_ref, red_ref):
    g = g_ref[...] / rows_total
    up, inv = factor_and_inverse(0.5 * (g + g.T))
    inv_t = inv.T
    h, m = split2(inv_t)
    hm = jnp.concatenate([h, m], axis=1)
    w1_ref[...] = jnp.concatenate([hm, hm], axis=0)
    fac_ref[...] = jnp.dot(up, up1_ref[...], precision=HIGH, preferred_element_type=F32)
    t = jnp.dot(inv, t_ref[...] / rows_total, precision=HIGH, preferred_element_type=F32)
    red_ref[...] = jnp.dot(t, inv_t, precision=HIGH, preferred_element_type=F32)


def chol2(g, t, up1, rows_total):
    k = g.shape[0]
    return pl.pallas_call(
        lambda *refs: chol2_kernel(rows_total, *refs),
        out_shape=(
            jax.ShapeDtypeStruct((2 * k, 2 * k), BF16),
            jax.ShapeDtypeStruct((k, k), F32),
            jax.ShapeDtypeStruct((k, k), F32),
        ),
        compiler_params=pltpu.CompilerParams(vmem_limit_bytes=VMEM_LIMIT),
        name="factor_second",
    )(g, t, up1)


def apply_blocks(cols_ref, jb_ref, source, width, store):
    block_rows, slots, blk, _ = jb_ref.shape
    start = cols_ref[0, 0]

    def body(r, carry):
        acc = jnp.zeros((blk, width), F32)
        for n in range(0, slots, 2):
            lhs = jnp.concatenate([jb_ref[r, n], jb_ref[r, n + 1]], axis=1)
            picked = []
            for p in (n, n + 1):
                index = cols_ref[r, p] - start + block_rows
                picked.append(source[rows_of(index, blk), :])
            acc = acc + mm(lhs, jnp.concatenate(picked, axis=0))
        store(r, acc)
        return carry

    lax.fori_loop(0, block_rows, body, 0, unroll=4)


def mid_kernel(cols_ref, before_ref, s_ref, after_ref, w1_ref, w2_ref, jb_ref, f_ref, g_ref, t_ref, y_ref):
    rows, k = s_ref.shape
    blk = jb_ref.shape[2]
    step = 256
    for part, ref in enumerate((before_ref, s_ref, after_ref)):

        def body(c, carry, ref=ref, part=part):
            h, m, l = split3(ref[rows_of(c, step), :])
            p = mm(jnp.concatenate([h, m], axis=1), w1_ref[...])
            q = mm(jnp.concatenate([h, l], axis=1), w2_ref[...])
            f = p[:, :k] + (p[:, k:] + q)
            f_ref[rows_of(c + part * (rows // step), step), :] = jnp.concatenate(split2(f), axis=1)
            return carry

        lax.fori_loop(0, rows // step, body, 0, unroll=4)

    def store(r, acc):
        y = acc[:, :k] + acc[:, k:]
        y_ref[rows_of(r, blk), :] = jnp.concatenate(split2(y), axis=1)

    apply_blocks(cols_ref, jb_ref, f_ref, 2 * k, store)

    def gram_body(c, acc):
        f = f_ref[rows_of(c + rows // step, step), :]
        y = y_ref[rows_of(c, step), :]
        acc = acc + mm_tn(f, jnp.concatenate([f[:, :k], y[:, :k]], axis=1))
        return acc + mm_tn(f, jnp.concatenate([f[:, k:], y[:, k:]], axis=1))

    acc = lax.fori_loop(0, rows // step, gram_body, jnp.zeros((2 * k, 2 * k), F32), unroll=4)
    acc = acc[:k, :] + acc[k:, :]
    g_ref[...] = acc[:, :k]
    t_ref[...] = acc[:, k:]


def mid(cols, before, s, after, w1, w2, jb):
    rows, k = s.shape
    vmem = pl.BlockSpec(memory_space=pltpu.VMEM)
    return pl.pallas_call(
        mid_kernel,
        in_specs=[pl.BlockSpec(memory_space=pltpu.SMEM)] + [vmem] * 6,
        out_specs=(vmem, vmem, vmem),
        out_shape=(
            jax.ShapeDtypeStruct((3 * rows, 2 * k), BF16),
            jax.ShapeDtypeStruct((k, k), F32),
            jax.ShapeDtypeStruct((k, k), F32),
        ),
        scratch_shapes=[pltpu.VMEM((rows, 2 * k), BF16)],
        compiler_params=pltpu.CompilerParams(vmem_limit_bytes=VMEM_LIMIT),
        name="first_and_sums",
    )(cols, before, s, after, w1, w2, jb)


def last_kernel(cols_ref, f_ref, w1_ref, jb_ref, modes_ref, jm_ref, mb_ref):
    rows, k = modes_ref.shape
    blk = jb_ref.shape[2]
    step = 256
    for part in range(3):

        def body(c, carry, part=part):
            at = rows_of(c + part * (rows // step), step)
            p = mm(f_ref[at, :], w1_ref[...])
            modes = p[:, :k] + p[:, k:]
            if part == 1:
                modes_ref[rows_of(c, step), :] = modes
            mb_ref[at, :] = modes.astype(BF16)
            return carry

        lax.fori_loop(0, rows // step, body, 0, unroll=4)

    def store(r, acc):
        jm_ref[rows_of(r, blk), :] = acc.astype(BF16)

    apply_blocks(cols_ref, jb_ref, mb_ref, k, store)


def last(cols, f, w1, jb):
    rows, k = f.shape[0] // 3, f.shape[1] // 2
    vmem = pl.BlockSpec(memory_space=pltpu.VMEM)
    return pl.pallas_call(
        last_kernel,
        in_specs=[pl.BlockSpec(memory_space=pltpu.SMEM)] + [vmem] * 3,
        out_specs=(vmem, vmem),
        out_shape=(
            jax.ShapeDtypeStruct((rows, k), F32),
            jax.ShapeDtypeStruct((rows, k), BF16),
        ),
        scratch_shapes=[pltpu.VMEM((3 * rows, k), BF16)],
        compiler_params=pltpu.CompilerParams(vmem_limit_bytes=VMEM_LIMIT),
        name="modes_and_apply",
    )(cols, f, w1, jb)


def solution(mesh):
    axes = tuple(mesh.axis_names)
    sizes = dict(mesh.shape)
    n_bulk, n_span = sizes["bulk"], sizes["span"]
    count = n_bulk * n_span
    weight = {"bulk": n_span, "span": 1} if axes[0] == "bulk" else {"bulk": 1, "span": n_bulk}
    bits = lambda n: [1 << i for i in range(n.bit_length() - 1)]
    core_mask = weight["bulk"]
    masks = [m * weight["span"] for m in bits(n_span)] + [m * weight["bulk"] for m in bits(n_bulk)[1:]]
    phases = [masks[i : i + 2] for i in range(0, len(masks), 2)]

    def swap(value, mask):
        return lax.ppermute(value, axes, [(i, i ^ mask) for i in range(count)])

    def sum_phases(value):
        for phase in phases:
            if len(phase) == 2:
                a, b = phase
                pa, pb, pab = swap(value, a), swap(value, b), swap(value, a | b)
                value = (value + pa) + (pb + pab)
            else:
                value = value + swap(value, phase[0])
        return value

    def shards(snapshots, jac_blocks, jac_cols):
        rows_total = snapshots.shape[0] * count
        up = [(i, i + 1) for i in range(n_bulk - 1)]
        down = [(i + 1, i) for i in range(n_bulk - 1)]
        before = lax.ppermute(snapshots, "bulk", up)
        after = lax.ppermute(snapshots, "bulk", down)
        gram = local_gram(snapshots)
        gram = sum_phases(gram + swap(gram, core_mask))
        up1, w1, w2 = chol1(gram, rows_total)
        f, g, t = mid(jac_cols, before, snapshots, after, w1, w2, jac_blocks)
        even = lax.axis_index("bulk") % 2 == 0
        mine = jnp.where(even, g, t) + swap(jnp.where(even, t, g), core_mask)
        mine = sum_phases(mine)
        other = swap(mine, core_mask)
        g, t = jnp.where(even, mine, other), jnp.where(even, other, mine)
        v1, factor, reduced = chol2(g, t, up1, rows_total)
        modes, jac_modes = last(jac_cols, f, v1, jac_blocks)
        return modes, factor, jac_modes, reduced

    rows = P(("span", "bulk"), None)
    return jax.shard_map(
        shards,
        mesh=mesh,
        in_specs=(rows, P(("span", "bulk"), None, None, None), rows),
        out_specs=(rows, P(), rows, P()),
        check_vma=False,
    )
```

```python
import jax
import jax.numpy as jnp
from jax import lax
from jax.experimental import pallas as pl
from jax.experimental.pallas import tpu as pltpu
from jax.sharding import PartitionSpec as P

F32 = jnp.float32
BF16 = jnp.bfloat16
HIGH = lax.Precision.HIGHEST
VMEM_LIMIT = 16 * 1024 * 1024


def mm(a, b):
    return lax.dot_general(a, b, (((1,), (0,)), ((), ())), preferred_element_type=F32)


def mm_tn(a, b):
    return lax.dot_general(a, b, (((0,), (0,)), ((), ())), preferred_element_type=F32)


def split2(x):
    h = x.astype(BF16)
    return h, (x - h.astype(F32)).astype(BF16)


def split3(x):
    h = x.astype(BF16)
    r = x - h.astype(F32)
    m = r.astype(BF16)
    return h, m, (r - m.astype(F32)).astype(BF16)


def rows_of(i, n):
    return pl.ds(pl.multiple_of(i * n, n), n)


def gram_kernel(s_ref, g_ref):
    rows, k = s_ref.shape
    step = 256
    hh = jnp.zeros((2 * k, 2 * k), F32)
    hl = jnp.zeros((k, k), F32)
    for c in range(rows // step):
        h, m, l = split3(s_ref[c * step : (c + 1) * step, :])
        hm = jnp.concatenate([h, m], axis=1)
        hh = hh + mm_tn(hm, hm)
        hl = hl + mm_tn(h, l)
    cross = hh[:k, k:] + hl
    g_ref[...] = hh[:k, :k] + (cross + cross.T + hh[k:, k:])


def local_gram(s):
    k = s.shape[1]
    return pl.pallas_call(
        gram_kernel,
        out_shape=jax.ShapeDtypeStruct((k, k), F32),
        compiler_params=pltpu.CompilerParams(vmem_limit_bytes=VMEM_LIMIT),
        name="local_gram",
    )(s)


def factor_and_inverse(a):
    k, n = a.shape[0], 8
    blocks = [a[n * i : n * i + n, :] for i in range(k // n)]
    lane = lax.broadcasted_iota(jnp.int32, (n, k), 1)
    sub = lax.broadcasted_iota(jnp.int32, (n, k), 0)
    full = lambda value: jnp.broadcast_to(value, (n, k))
    for p in range(k // n):
        x = blocks[p]
        at = n * p
        columns = [full(x[:, at + t : at + t + 1]) for t in range(n)]
        d = {(s, t): full(columns[t][s : s + 1, :]) for t in range(n) for s in range(t, n)}
        row = [full(x[s : s + 1, :]) for s in range(n)]
        done, scale, low = [], [], {}
        for t in range(n):
            scale.append(lax.rsqrt(d[t, t]))
            here = lane == at + t
            done.append(jnp.where(here, scale[t], row[t] * scale[t]))
            for s in range(t + 1, n):
                low[s, t] = d[s, t] * scale[t]
            for u in range(t + 1, n):
                for s in range(u, n):
                    d[s, u] = d[s, u] - low[s, t] * low[u, t]
            for s in range(t + 1, n):
                row[s] = jnp.where(here, 0.0, row[s]) - low[s, t] * done[t]
        out = done[0]
        for t in range(1, n):
            out = jnp.where(sub == t, done[t], out)
        blocks[p] = out
        panel = (lane >= at) & (lane < at + n)
        terms = [jnp.where(panel & (lane > at + t), 0.0, done[t]) for t in range(n)]
        for i in range(p + 1, k // n):
            x = blocks[i]
            new = jnp.where(panel, 0.0, x)
            column = []
            for t in range(n):
                c = full(x[:, at + t : at + t + 1])
                for u in range(t):
                    c = c - column[u] * low[t, u]
                column.append(c * scale[t])
                new = new - column[t] * terms[t]
            blocks[i] = new
    x = jnp.concatenate(blocks, axis=0)
    r = lax.broadcasted_iota(jnp.int32, (k, k), 0)
    c = lax.broadcasted_iota(jnp.int32, (k, k), 1)
    upper = jnp.where(c > r, x, jnp.where(c == r, 1.0 / x, 0.0))
    return upper, jnp.where(c <= r, x, 0.0)


def chol1_kernel(rows_total, g_ref, up_ref, w1_ref, w2_ref):
    k = g_ref.shape[0]
    g = g_ref[...] / rows_total
    up, inv = factor_and_inverse(0.5 * (g + g.T))
    up_ref[...] = up
    h, m, l = split3(inv.T)
    hm = jnp.concatenate([h, m], axis=1)
    w1_ref[...] = jnp.concatenate([hm, hm], axis=0)
    w2_ref[...] = jnp.concatenate([l, h], axis=0)


def chol1(g, rows_total):
    k = g.shape[0]
    return pl.pallas_call(
        lambda *refs: chol1_kernel(rows_total, *refs),
        out_shape=(
            jax.ShapeDtypeStruct((k, k), F32),
            jax.ShapeDtypeStruct((2 * k, 2 * k), BF16),
            jax.ShapeDtypeStruct((2 * k, k), BF16),
        ),
        compiler_params=pltpu.CompilerParams(vmem_limit_bytes=VMEM_LIMIT),
        name="factor_first",
    )(g)


def chol2_kernel(rows_total, g_ref, t_ref, up1_ref, w1_ref, fac_ref, red_ref):
    g = g_ref[...] / rows_total
    up, inv = factor_and_inverse(0.5 * (g + g.T))
    inv_t = inv.T
    h, m = split2(inv_t)
    hm = jnp.concatenate([h, m], axis=1)
    w1_ref[...] = jnp.concatenate([hm, hm], axis=0)
    fac_ref[...] = jnp.dot(up, up1_ref[...], precision=HIGH, preferred_element_type=F32)
    t = jnp.dot(inv, t_ref[...] / rows_total, precision=HIGH, preferred_element_type=F32)
    red_ref[...] = jnp.dot(t, inv_t, precision=HIGH, preferred_element_type=F32)


def chol2(g, t, up1, rows_total):
    k = g.shape[0]
    return pl.pallas_call(
        lambda *refs: chol2_kernel(rows_total, *refs),
        out_shape=(
            jax.ShapeDtypeStruct((2 * k, 2 * k), BF16),
            jax.ShapeDtypeStruct((k, k), F32),
            jax.ShapeDtypeStruct((k, k), F32),
        ),
        compiler_params=pltpu.CompilerParams(vmem_limit_bytes=VMEM_LIMIT),
        name="factor_second",
    )(g, t, up1)


def apply_blocks(cols_ref, jb_ref, source, width, store):
    block_rows, slots, blk, _ = jb_ref.shape
    start = cols_ref[0, 0]

    def body(r, carry):
        acc = jnp.zeros((blk, width), F32)
        for n in range(0, slots, 2):
            lhs = jnp.concatenate([jb_ref[r, n], jb_ref[r, n + 1]], axis=1)
            picked = []
            for p in (n, n + 1):
                index = cols_ref[r, p] - start + block_rows
                picked.append(source[rows_of(index, blk), :])
            acc = acc + mm(lhs, jnp.concatenate(picked, axis=0))
        store(r, acc)
        return carry

    lax.fori_loop(0, block_rows, body, 0, unroll=4)


def mid_kernel(cols_ref, before_ref, s_ref, after_ref, w1_ref, w2_ref, jb_ref, f_ref, g_ref, t_ref, y_ref):
    rows, k = s_ref.shape
    blk = jb_ref.shape[2]
    step = 256
    for part, ref in enumerate((before_ref, s_ref, after_ref)):

        def body(c, carry, ref=ref, part=part):
            h, m, l = split3(ref[rows_of(c, step), :])
            p = mm(jnp.concatenate([h, m], axis=1), w1_ref[...])
            q = mm(jnp.concatenate([h, l], axis=1), w2_ref[...])
            f = p[:, :k] + (p[:, k:] + q)
            f_ref[rows_of(c + part * (rows // step), step), :] = jnp.concatenate(split2(f), axis=1)
            return carry

        lax.fori_loop(0, rows // step, body, 0, unroll=4)

    def store(r, acc):
        y = acc[:, :k] + acc[:, k:]
        y_ref[rows_of(r, blk), :] = jnp.concatenate(split2(y), axis=1)

    apply_blocks(cols_ref, jb_ref, f_ref, 2 * k, store)

    def gram_body(c, acc):
        f = f_ref[rows_of(c + rows // step, step), :]
        y = y_ref[rows_of(c, step), :]
        acc = acc + mm_tn(f, jnp.concatenate([f[:, :k], y[:, :k]], axis=1))
        return acc + mm_tn(f, jnp.concatenate([f[:, k:], y[:, k:]], axis=1))

    acc = lax.fori_loop(0, rows // step, gram_body, jnp.zeros((2 * k, 2 * k), F32), unroll=4)
    acc = acc[:k, :] + acc[k:, :]
    g_ref[...] = acc[:, :k]
    t_ref[...] = acc[:, k:]


def mid(cols, before, s, after, w1, w2, jb):
    rows, k = s.shape
    vmem = pl.BlockSpec(memory_space=pltpu.VMEM)
    return pl.pallas_call(
        mid_kernel,
        in_specs=[pl.BlockSpec(memory_space=pltpu.SMEM)] + [vmem] * 6,
        out_specs=(vmem, vmem, vmem),
        out_shape=(
            jax.ShapeDtypeStruct((3 * rows, 2 * k), BF16),
            jax.ShapeDtypeStruct((k, k), F32),
            jax.ShapeDtypeStruct((k, k), F32),
        ),
        scratch_shapes=[pltpu.VMEM((rows, 2 * k), BF16)],
        compiler_params=pltpu.CompilerParams(vmem_limit_bytes=VMEM_LIMIT),
        name="first_and_sums",
    )(cols, before, s, after, w1, w2, jb)


def last_kernel(cols_ref, f_ref, w1_ref, jb_ref, modes_ref, jm_ref, mb_ref):
    rows, k = modes_ref.shape
    blk = jb_ref.shape[2]
    step = 256
    for part in range(3):

        def body(c, carry, part=part):
            at = rows_of(c + part * (rows // step), step)
            p = mm(f_ref[at, :], w1_ref[...])
            modes = p[:, :k] + p[:, k:]
            if part == 1:
                modes_ref[rows_of(c, step), :] = modes
            mb_ref[at, :] = modes.astype(BF16)
            return carry

        lax.fori_loop(0, rows // step, body, 0, unroll=4)

    def store(r, acc):
        jm_ref[rows_of(r, blk), :] = acc.astype(BF16)

    apply_blocks(cols_ref, jb_ref, mb_ref, k, store)


def last(cols, f, w1, jb):
    rows, k = f.shape[0] // 3, f.shape[1] // 2
    vmem = pl.BlockSpec(memory_space=pltpu.VMEM)
    return pl.pallas_call(
        last_kernel,
        in_specs=[pl.BlockSpec(memory_space=pltpu.SMEM)] + [vmem] * 3,
        out_specs=(vmem, vmem),
        out_shape=(
            jax.ShapeDtypeStruct((rows, k), F32),
            jax.ShapeDtypeStruct((rows, k), BF16),
        ),
        scratch_shapes=[pltpu.VMEM((3 * rows, k), BF16)],
        compiler_params=pltpu.CompilerParams(vmem_limit_bytes=VMEM_LIMIT),
        name="modes_and_apply",
    )(cols, f, w1, jb)


def solution(mesh):
    axes = tuple(mesh.axis_names)
    sizes = dict(mesh.shape)
    n_bulk, n_span = sizes["bulk"], sizes["span"]
    count = n_bulk * n_span
    weight = {"bulk": n_span, "span": 1} if axes[0] == "bulk" else {"bulk": 1, "span": n_bulk}
    bits = lambda n: [1 << i for i in range(n.bit_length() - 1)]
    core_mask = weight["bulk"]
    masks = [m * weight["span"] for m in bits(n_span)] + [m * weight["bulk"] for m in bits(n_bulk)[1:]]
    phases = [masks[i : i + 2] for i in range(0, len(masks), 2)]

    def swap(value, mask):
        return lax.ppermute(value, axes, [(i, i ^ mask) for i in range(count)])

    def sum_phases(value, phases):
        for phase in phases:
            if len(phase) == 2:
                a, b = phase
                pa, pb, pab = swap(value, a), swap(value, b), swap(value, a | b)
                value = (value + pa) + (pb + pab)
            else:
                value = value + swap(value, phase[0])
        return value

    def shards(snapshots, jac_blocks, jac_cols):
        rows_total = snapshots.shape[0] * count
        up = [(i, i + 1) for i in range(n_bulk - 1)]
        down = [(i + 1, i) for i in range(n_bulk - 1)]
        before = lax.ppermute(snapshots, "bulk", up)
        after = lax.ppermute(snapshots, "bulk", down)
        gram = local_gram(snapshots)
        gram = sum_phases(gram + swap(gram, core_mask), phases[::-1])
        up1, w1, w2 = chol1(gram, rows_total)
        f, g, t = mid(jac_cols, before, snapshots, after, w1, w2, jac_blocks)
        even = lax.axis_index("bulk") % 2 == 0
        mine = jnp.where(even, g, t) + swap(jnp.where(even, t, g), core_mask)
        mine = sum_phases(mine, phases)
        other = swap(mine, core_mask)
        g, t = jnp.where(even, mine, other), jnp.where(even, other, mine)
        v1, factor, reduced = chol2(g, t, up1, rows_total)
        modes, jac_modes = last(jac_cols, f, v1, jac_blocks)
        return modes, factor, jac_modes, reduced

    rows = P(("span", "bulk"), None)
    return jax.shard_map(
        shards,
        mesh=mesh,
        in_specs=(rows, P(("span", "bulk"), None, None, None), rows),
        out_specs=(rows, P(), rows, P()),
        check_vma=False,
    )
```

```python
import math

import jax
import jax.numpy as jnp
from jax import lax
from jax.experimental import pallas as pl
from jax.experimental.pallas import tpu as pltpu
from jax.sharding import PartitionSpec as P

F32 = jnp.float32
BF16 = jnp.bfloat16
HIGH = lax.Precision.HIGHEST
VMEM_LIMIT = 24 * 1024 * 1024
CHUNK = 512
TILE = 256


def mm(a, b, contract=(1, 0)):
    return lax.dot_general(a, b, (((contract[0],), (contract[1],)), ((), ())), preferred_element_type=F32)


def split2(x):
    h = x.astype(BF16)
    return h, (x - h.astype(F32)).astype(BF16)


def split3(x):
    h = x.astype(BF16)
    r = x - h.astype(F32)
    m = r.astype(BF16)
    return h, m, (r - m.astype(F32)).astype(BF16)


def rows_of(i, n):
    return pl.ds(pl.multiple_of(i * n, n), n)


def two_sum(a, b):
    s = a + b
    t = s - a
    return s, (a - (s - t)) + (b - t)


def descending(terms):
    high, low = terms[0], jnp.zeros_like(terms[0])
    for term in terms[1:]:
        high, error = two_sum(high, term)
        low = low + error
    return high, low


def add_pairs(a, b):
    high, error = two_sum(a[0], b[0])
    low = (a[1] + b[1]) + error
    total = high + low
    return jnp.stack([total, low - (total - high)])


def power_of_two(x):
    q = x * float(2**23 + 1)
    return 2.0 * jnp.abs(q - q * (1.0 - 2.0**-24))


def cut(x, size, n):
    grid = size * (1.5 * 2.0**16)
    parts = []
    for _ in range(n):
        part = (x + grid) - grid
        x = x - part
        parts.append(part.astype(BF16))
        grid = grid * 2.0**-8
    return parts, x


def gram_kernel(s_hbm, g_ref, s_ref, sem):
    rows, k = s_ref.shape
    chunks = rows // CHUNK
    copies = [
        pltpu.make_async_copy(s_hbm.at[pl.ds(c * CHUNK, CHUNK)], s_ref.at[pl.ds(c * CHUNK, CHUNK)], sem.at[c])
        for c in range(chunks)
    ]
    for copy in copies:
        copy.start()
    top = jnp.zeros((8, k), F32)
    for c, copy in enumerate(copies):
        copy.wait()
        rows_here = jnp.abs(s_ref[c * CHUNK : (c + 1) * CHUNK, :])
        top = jnp.maximum(top, jnp.max(rows_here.reshape(CHUNK // 8, 8, k), axis=0))
    size = power_of_two(jnp.max(top, axis=0, keepdims=True))
    zero = jnp.zeros((k, k), F32)
    aa, aa_low, ab, ab_low, odd, even = zero, zero, zero, zero, zero, zero
    for c in range(chunks):
        one, two, three = jnp.zeros((k, 2 * k), F32), jnp.zeros((2 * k, 2 * k), F32), zero
        for at in range(c * CHUNK, (c + 1) * CHUNK, TILE):
            (p, q, r), _ = cut(s_ref[at : at + TILE, :], size, 3)
            pq = jnp.concatenate([p, q], axis=1)
            one = one + mm(p, pq, (0, 0))
            two = two + mm(pq, jnp.concatenate([r, q], axis=1), (0, 0))
            three = three + mm(r, r, (0, 0))
        aa, error = two_sum(aa, one[:, :k])
        aa_low = aa_low + error
        ab, error = two_sum(ab, one[:, k:])
        ab_low = ab_low + error
        odd = odd + (two[:k, :k] + two[k:, :k])
        even = even + (two[k:, k:] + three)
    cross, cross_low = two_sum(ab, ab.T)
    total, total_low = two_sum(aa, cross)
    low = ab_low + (odd + 0.5 * even)
    low = (aa_low + (cross_low + total_low)) + (low + low.T)
    high = total + low
    g_ref[0] = high
    g_ref[1] = low - (high - total)


def local_gram(s):
    rows, k = s.shape
    return pl.pallas_call(
        gram_kernel,
        in_specs=[pl.BlockSpec(memory_space=pl.ANY)],
        out_shape=jax.ShapeDtypeStruct((2, k, k), F32),
        scratch_shapes=[pltpu.VMEM((rows, k), F32), pltpu.SemaphoreType.DMA((rows // CHUNK,))],
        compiler_params=pltpu.CompilerParams(vmem_limit_bytes=VMEM_LIMIT),
        name="local_gram",
    )(s)


def factor_and_inverse(a):
    k, n = a.shape[0], 8
    blocks = [a[n * i : n * i + n, :] for i in range(k // n)]
    lane = lax.broadcasted_iota(jnp.int32, (n, k), 1)
    sub = lax.broadcasted_iota(jnp.int32, (n, k), 0)
    full = lambda value: jnp.broadcast_to(value, (n, k))
    for p in range(k // n):
        x = blocks[p]
        at = n * p
        columns = [full(x[:, at + t : at + t + 1]) for t in range(n)]
        d = {(s, t): full(columns[t][s : s + 1, :]) for t in range(n) for s in range(t, n)}
        row = [full(x[s : s + 1, :]) for s in range(n)]
        done, scale, low = [], [], {}
        for t in range(n):
            scale.append(lax.rsqrt(d[t, t]))
            here = lane == at + t
            done.append(jnp.where(here, scale[t], row[t] * scale[t]))
            for s in range(t + 1, n):
                low[s, t] = d[s, t] * scale[t]
            for u in range(t + 1, n):
                for s in range(u, n):
                    d[s, u] = d[s, u] - low[s, t] * low[u, t]
            for s in range(t + 1, n):
                row[s] = jnp.where(here, 0.0, row[s]) - low[s, t] * done[t]
        out = done[0]
        for t in range(1, n):
            out = jnp.where(sub == t, done[t], out)
        blocks[p] = out
        panel = (lane >= at) & (lane < at + n)
        terms = [jnp.where(panel & (lane > at + t), 0.0, done[t]) for t in range(n)]
        for i in range(p + 1, k // n):
            x = blocks[i]
            new = jnp.where(panel, 0.0, x)
            column = []
            for t in range(n):
                c = full(x[:, at + t : at + t + 1])
                for u in range(t):
                    c = c - column[u] * low[t, u]
                column.append(c * scale[t])
                new = new - column[t] * terms[t]
            blocks[i] = new
    x = jnp.concatenate(blocks, axis=0)
    r = lax.broadcasted_iota(jnp.int32, (k, k), 0)
    c = lax.broadcasted_iota(jnp.int32, (k, k), 1)
    upper = jnp.where(c > r, x, jnp.where(c == r, 1.0 / x, 0.0))
    return upper, jnp.where(c <= r, x, 0.0)


def scaled(high, low):
    k = high.shape[0]
    r = lax.broadcasted_iota(jnp.int32, (k, k), 0)
    c = lax.broadcasted_iota(jnp.int32, (k, k), 1)
    diagonal = jnp.where(r == c, high, 0.0)
    row = power_of_two(jnp.sqrt(jnp.max(diagonal, axis=0, keepdims=True)))
    col = power_of_two(jnp.sqrt(jnp.max(diagonal, axis=1, keepdims=True)))
    return (high / row) / col, (low / row) / col, row


def by_weight(products, k, n, m):
    block = lambda i, j: products[i * k : (i + 1) * k, j * k : (j + 1) * k]
    return [sum(block(i, t - i) for i in range(n) if 0 <= t - i < m) for t in range(n + m - 1)]


def factors_kernel(count, g_ref, up_ref, w1_ref, w2_ref):
    k = g_ref.shape[1]
    high, low, row = scaled(g_ref[0], g_ref[1])
    up1, inv1 = factor_and_inverse(0.5 * (high + high.T))
    size = power_of_two(jnp.max(jnp.abs(inv1), axis=1, keepdims=True))
    p, left = cut(inv1, size, 3)
    inv1 = inv1 - left
    g, left = cut(high, 1.0, 3)
    g += cut(left + low, 2.0**-24, 2)[0]
    p_rows = jnp.concatenate(p, axis=0)
    y, y_low = descending(by_weight(mm(p_rows, jnp.concatenate(g, axis=1)), k, 3, 5))
    size = power_of_two(jnp.max(jnp.abs(y), axis=1, keepdims=True))
    y, left = cut(y, size, 3)
    y += cut(left + y_low, size * 2.0**-24, 1)[0]
    gram2, low = descending(by_weight(mm(jnp.concatenate(y, axis=0), p_rows, (1, 1)), k, 4, 3))
    gram2 = gram2 + low
    up2, inv2 = factor_and_inverse(0.5 * (gram2 + gram2.T))
    inverse = jnp.dot(inv2, inv1, precision=HIGH, preferred_element_type=F32)
    inverse = (inverse / row) * math.sqrt(count)
    h, m, l = split3(inverse.T)
    hm = jnp.concatenate([h, m], axis=1)
    w1_ref[...] = jnp.concatenate([hm, hm], axis=0)
    w2_ref[...] = jnp.concatenate([l, h], axis=0)
    upper = jnp.dot(up2, up1, precision=HIGH, preferred_element_type=F32)
    up_ref[...] = (upper * row) / math.sqrt(count)


def factors(g, count):
    k = g.shape[1]
    return pl.pallas_call(
        lambda *refs: factors_kernel(count, *refs),
        out_shape=(
            jax.ShapeDtypeStruct((k, k), F32),
            jax.ShapeDtypeStruct((2 * k, 2 * k), BF16),
            jax.ShapeDtypeStruct((2 * k, k), BF16),
        ),
        compiler_params=pltpu.CompilerParams(vmem_limit_bytes=VMEM_LIMIT),
        name="factors",
    )(g)


def last_kernel(
    cols_ref, s_hbm, chip_hbm, inner_hbm, outer_hbm, w1_ref, w2_ref, jb_hbm, modes_hbm, jm_hbm, red_ref,
    s_ref, jb_ref, modes_ref, jm_ref, mb_ref, hm_ref, sem,
):
    _, rows, k = s_ref.shape
    block_rows, slots, blk, _ = jb_ref.shape
    per = rows // TILE
    place = lax.axis_index("bulk")
    get = [pltpu.make_async_copy(ref, s_ref.at[i], sem.at[i]) for i, ref in enumerate((s_hbm, chip_hbm, inner_hbm))]
    get_outer = pltpu.make_async_copy(outer_hbm, s_ref.at[2], sem.at[2])
    get_jb = pltpu.make_async_copy(jb_hbm, jb_ref, sem.at[3])
    put_modes = pltpu.make_async_copy(modes_ref, modes_hbm, sem.at[4])
    put_jm = pltpu.make_async_copy(jm_ref, jm_hbm, sem.at[5])
    is_inner = (place % 4 == 1) | (place % 4 == 2)
    get[0].start()
    get[1].start()

    @pl.when(is_inner)
    def _():
        get[2].start()

    @pl.when(jnp.logical_not(is_inner))
    def _():
        get_outer.start()

    get_jb.start()
    odd = place % 2
    offsets = (per, (2 - 2 * odd) * per, 2 * odd * per)

    for part, offset in enumerate(offsets):
        get[part].wait()

        def body(c, carry, part=part, offset=offset):
            h, m, l = split3(s_ref[part, rows_of(c, TILE), :])
            p = mm(jnp.concatenate([h, m], axis=1), w1_ref[...])
            q = mm(jnp.concatenate([h, l], axis=1), w2_ref[...])
            modes = p[:, :k] + (p[:, k:] + q)
            high, low = split2(modes)
            mb_ref[rows_of(c + offset, TILE), :] = high
            if part == 0:
                modes_ref[rows_of(c, TILE), :] = modes
                hm_ref[rows_of(c, TILE), :] = jnp.concatenate([high, low], axis=1)
            return carry

        lax.fori_loop(0, per, body, 0, unroll=4)
        if part == 0:
            put_modes.start()

    get_jb.wait()
    start = cols_ref[0, 0]

    def apply(r, carry):
        acc = jnp.zeros((blk, k), F32)
        for n in range(0, slots, 2):
            lhs = jnp.concatenate([jb_ref[r, n], jb_ref[r, n + 1]], axis=1)
            picked = []
            for p in (n, n + 1):
                index = cols_ref[r, p] - start + block_rows
                picked.append(mb_ref[rows_of(index, blk), :])
            acc = acc + mm(lhs, jnp.concatenate(picked, axis=0))
        jm_ref[rows_of(r, blk), :] = acc.astype(BF16)
        return carry

    lax.fori_loop(0, block_rows, apply, 0, unroll=4)
    put_jm.start()

    def project(c, acc):
        at = rows_of(c, TILE)
        return acc + mm(hm_ref[at, :], jm_ref[at, :], (0, 0))

    acc = lax.fori_loop(0, per, project, jnp.zeros((2 * k, k), F32), unroll=4)
    red_ref[...] = acc[:k, :] + acc[k:, :]
    put_modes.wait()
    put_jm.wait()


def last(cols, s, chip, inner, outer, w1, w2, jb):
    rows, k = s.shape
    vmem, hbm = pl.BlockSpec(memory_space=pltpu.VMEM), pl.BlockSpec(memory_space=pl.ANY)
    return pl.pallas_call(
        last_kernel,
        in_specs=[pl.BlockSpec(memory_space=pltpu.SMEM)] + [hbm] * 4 + [vmem] * 2 + [hbm],
        out_specs=(hbm, hbm, vmem),
        out_shape=(
            jax.ShapeDtypeStruct((rows, k), F32),
            jax.ShapeDtypeStruct((rows, k), BF16),
            jax.ShapeDtypeStruct((k, k), F32),
        ),
        scratch_shapes=[
            pltpu.VMEM((3, rows, k), F32),
            pltpu.VMEM(jb.shape, BF16),
            pltpu.VMEM((rows, k), F32),
            pltpu.VMEM((rows, k), BF16),
            pltpu.VMEM((3 * rows, k), BF16),
            pltpu.VMEM((rows, 2 * k), BF16),
            pltpu.SemaphoreType.DMA((6,)),
        ],
        compiler_params=pltpu.CompilerParams(vmem_limit_bytes=VMEM_LIMIT),
        name="modes_and_apply",
    )(cols, s, chip, inner, outer, w1, w2, jb)


def solution(mesh):
    axes = tuple(mesh.axis_names)
    sizes = dict(mesh.shape)
    n_bulk, n_span = sizes["bulk"], sizes["span"]
    count = n_bulk * n_span
    weight = {"bulk": n_span, "span": 1} if axes[0] == "bulk" else {"bulk": 1, "span": n_bulk}
    bits = lambda n: [1 << i for i in range(n.bit_length() - 1)]
    core_mask = weight["bulk"]
    masks = [m * weight["span"] for m in bits(n_span)] + [m * weight["bulk"] for m in bits(n_bulk)[1:]]
    phases = [masks[i : i + 2] for i in range(0, len(masks), 2)]
    masks_x, masks_y = [core_mask * 2], masks[:1]
    others = [m for m in masks if m not in masks_x + masks_y]
    masks_far = [others[i : i + 2] for i in range(0, len(others), 2)]

    def swap(value, mask):
        return lax.ppermute(value, axes, [(i, i ^ mask) for i in range(count)])

    def exchange(value, phase, add):
        if len(phase) == 1:
            return add(value, swap(value, phase[0]))
        a, b = phase
        pa, pb, pab = swap(value, a), swap(value, b), swap(value, a | b)
        return add(add(value, pa), add(pb, pab))

    def shards(snapshots, jac_blocks, jac_cols):
        rows_total = snapshots.shape[0] * count
        even = lax.axis_index("bulk") % 2 == 0
        pairs = lambda first: [p for i in range(first, n_bulk - 1, 4) for p in ((i, i + 1), (i + 1, i))]
        chip = swap(snapshots, core_mask)
        inner = lax.ppermute(snapshots, "bulk", pairs(1))
        gram = local_gram(snapshots)
        half = gram.shape[1] // 2
        upper, lower = gram[:, :half], gram[:, half:]
        mine = add_pairs(jnp.where(even, upper, lower), swap(jnp.where(even, lower, upper), core_mask))
        for phase in masks_far:
            mine = exchange(mine, phase, add_pairs)
        mine, inner = lax.optimization_barrier((mine, inner))
        mine = exchange(mine, masks_x, add_pairs)
        mine, late = lax.optimization_barrier((mine, snapshots))
        outer = lax.ppermute(late, "bulk", pairs(3))
        mine = exchange(mine, masks_y, add_pairs)
        other = swap(mine, core_mask)
        gram = jnp.concatenate([jnp.where(even, mine, other), jnp.where(even, other, mine)], axis=1)
        factor, w1, w2 = factors(gram, rows_total)
        modes, jac_modes, reduced = last(jac_cols, snapshots, chip, inner, outer, w1, w2, jac_blocks)
        reduced = reduced + swap(reduced, core_mask)
        for phase in phases:
            reduced = exchange(reduced, phase, jnp.add)
        return modes, factor, jac_modes, reduced / rows_total

    rows = P(("span", "bulk"), None)
    return jax.shard_map(
        shards,
        mesh=mesh,
        in_specs=(rows, P(("span", "bulk"), None, None, None), rows),
        out_specs=(rows, P(), rows, P()),
        check_vma=False,
    )
```

```python
import math

import jax
import jax.numpy as jnp
from jax import lax
from jax.experimental import pallas as pl
from jax.experimental.pallas import tpu as pltpu
from jax.sharding import PartitionSpec as P

F32 = jnp.float32
BF16 = jnp.bfloat16
HIGH = lax.Precision.HIGHEST
VMEM_LIMIT = 24 * 1024 * 1024
CHUNK = 512
TILE = 256


def mm(a, b, contract=(1, 0)):
    return lax.dot_general(a, b, (((contract[0],), (contract[1],)), ((), ())), preferred_element_type=F32)


def split2(x):
    h = x.astype(BF16)
    return h, (x - h.astype(F32)).astype(BF16)


def split3(x):
    h = x.astype(BF16)
    r = x - h.astype(F32)
    m = r.astype(BF16)
    return h, m, (r - m.astype(F32)).astype(BF16)


def in_vmem(x):
    return pltpu.with_memory_space_constraint(x, pltpu.VMEM)


def rows_of(i, n):
    return pl.ds(pl.multiple_of(i * n, n), n)


def two_sum(a, b):
    s = a + b
    t = s - a
    return s, (a - (s - t)) + (b - t)


def descending(terms):
    high, low = terms[0], jnp.zeros_like(terms[0])
    for term in terms[1:]:
        high, error = two_sum(high, term)
        low = low + error
    return high, low


def add_pairs(a, b):
    high, error = two_sum(a[0], b[0])
    low = (a[1] + b[1]) + error
    total = high + low
    return jnp.stack([total, low - (total - high)])


def power_of_two(x):
    q = x * float(2**23 + 1)
    return 2.0 * jnp.abs(q - q * (1.0 - 2.0**-24))


def cut(x, size, n):
    grid = size * (1.5 * 2.0**16)
    parts = []
    for _ in range(n):
        part = (x + grid) - grid
        x = x - part
        parts.append(part.astype(BF16))
        grid = grid * 2.0**-8
    return parts, x


def gram_kernel(s_hbm, g_ref, s_ref, sem):
    rows, k = s_ref.shape
    chunks = rows // CHUNK
    copies = [
        pltpu.make_async_copy(s_hbm.at[pl.ds(c * CHUNK, CHUNK)], s_ref.at[pl.ds(c * CHUNK, CHUNK)], sem.at[c])
        for c in range(chunks)
    ]
    for copy in copies:
        copy.start()
    top = jnp.zeros((8, k), F32)
    for c, copy in enumerate(copies):
        copy.wait()
        rows_here = jnp.abs(s_ref[c * CHUNK : (c + 1) * CHUNK, :])
        top = jnp.maximum(top, jnp.max(rows_here.reshape(CHUNK // 8, 8, k), axis=0))
    size = power_of_two(jnp.max(top, axis=0, keepdims=True))
    zero = jnp.zeros((k, k), F32)
    aa, aa_low, ab, ab_low, odd, even = zero, zero, zero, zero, zero, zero
    for c in range(chunks):
        one, two, three = jnp.zeros((k, 2 * k), F32), jnp.zeros((2 * k, 2 * k), F32), zero
        for at in range(c * CHUNK, (c + 1) * CHUNK, TILE):
            (p, q, r), _ = cut(s_ref[at : at + TILE, :], size, 3)
            pq = jnp.concatenate([p, q], axis=1)
            one = one + mm(p, pq, (0, 0))
            two = two + mm(pq, jnp.concatenate([r, q], axis=1), (0, 0))
            three = three + mm(r, r, (0, 0))
        aa, error = two_sum(aa, one[:, :k])
        aa_low = aa_low + error
        ab, error = two_sum(ab, one[:, k:])
        ab_low = ab_low + error
        odd = odd + (two[:k, :k] + two[k:, :k])
        even = even + (two[k:, k:] + three)
    cross, cross_low = two_sum(ab, ab.T)
    total, total_low = two_sum(aa, cross)
    low = ab_low + (odd + 0.5 * even)
    low = (aa_low + (cross_low + total_low)) + (low + low.T)
    high = total + low
    g_ref[0] = high
    g_ref[1] = low - (high - total)


def local_gram(s):
    rows, k = s.shape
    return pl.pallas_call(
        gram_kernel,
        in_specs=[pl.BlockSpec(memory_space=pl.ANY)],
        out_shape=jax.ShapeDtypeStruct((2, k, k), F32),
        scratch_shapes=[pltpu.VMEM((rows, k), F32), pltpu.SemaphoreType.DMA((rows // CHUNK,))],
        compiler_params=pltpu.CompilerParams(vmem_limit_bytes=VMEM_LIMIT),
        name="local_gram",
    )(s)


def inverse_factor(a):
    k, n = a.shape[0], 8
    blocks = [a[n * i : n * i + n, :] for i in range(k // n)]
    lane = lax.broadcasted_iota(jnp.int32, (n, k), 1)
    sub = lax.broadcasted_iota(jnp.int32, (n, k), 0)
    full = lambda value: jnp.broadcast_to(value, (n, k))
    column_of = lambda x, j: full(x[:, j : j + 1])
    row_of = lambda x, s: full(x[s : s + 1, :])
    below = [(s, t) for t in range(n) for s in range(t, n)]
    first = [column_of(blocks[0], t) for t in range(n)]
    d = {(s, t): row_of(first[t], s) for s, t in below}
    rows = []
    for p in range(k // n):
        at = n * p
        row = [row_of(blocks[p], s) for s in range(n)]
        done, scale, low = [], [], {}
        for t in range(n):
            scale.append(lax.rsqrt(d[t, t]))
            here = lane == at + t
            done.append(jnp.where(here, scale[t], row[t] * scale[t]))
            for s in range(t + 1, n):
                low[s, t] = d[s, t] * scale[t]
            for u in range(t + 1, n):
                for s in range(u, n):
                    d[s, u] = d[s, u] - low[s, t] * low[u, t]
            for s in range(t + 1, n):
                row[s] = jnp.where(here, 0.0, row[s]) - low[s, t] * done[t]
        out = done[0]
        for t in range(1, n):
            out = jnp.where(sub == t, done[t], out)
        rows.append(out)
        panel = (lane >= at) & (lane < at + n)
        terms = [jnp.where(panel & (lane > at + t), 0.0, done[t]) for t in range(n)]
        for i in range(p + 1, k // n):
            x = blocks[i]
            new = jnp.where(panel, 0.0, x)
            column = []
            for t in range(n):
                c = column_of(x, at + t)
                for u in range(t):
                    c = c - column[u] * low[t, u]
                column.append(c * scale[t])
                new = new - column[t] * terms[t]
            blocks[i] = new
            if i == p + 1:
                ahead = [column_of(x, at + n + s) for s in range(n)]
                parts = [[row_of(c, s) for s in range(n)] for c in column]
                for t in range(n - 1):
                    for s in range(n):
                        ahead[s] = ahead[s] - column[t] * parts[t][s]
                last = parts[n - 1]
                d = {(s, t): row_of(ahead[t], s) - last[s] * last[t] for s, t in below}
    x = jnp.concatenate(rows, axis=0)
    r = lax.broadcasted_iota(jnp.int32, (k, k), 0)
    c = lax.broadcasted_iota(jnp.int32, (k, k), 1)
    return jnp.where(c <= r, x, 0.0)


def mm3(a, b, contract=(1, 0)):
    ah, am = split2(a)
    bh, bm = split2(b)
    return mm(ah, bh, contract) + (mm(ah, bm, contract) + mm(am, bh, contract))


def inverse_factor_near_one(e):
    k = e.shape[0]
    r = lax.broadcasted_iota(jnp.int32, (k, k), 0)
    c = lax.broadcasted_iota(jnp.int32, (k, k), 1)
    half = lambda x: jnp.where(c < r, x, jnp.where(c == r, 0.5 * x, 0.0))
    f = half(e)
    ff = mm3(f, f)
    n = half(mm3(f, f, (1, 1)) + (ff + ff.T)) - f
    ne = mm3(n, e)
    left = (e + (n + n.T)) + ((ne + ne.T) + mm3(n + ne, n, (1, 1)))
    step = half(left)
    return jnp.where(c == r, 1.0, 0.0) + (n - (step + mm3(step, n)))


def scaled(high, low):
    k = high.shape[0]
    r = lax.broadcasted_iota(jnp.int32, (k, k), 0)
    c = lax.broadcasted_iota(jnp.int32, (k, k), 1)
    diagonal = jnp.where(r == c, high, 0.0)
    row = power_of_two(jnp.sqrt(jnp.max(diagonal, axis=0, keepdims=True)))
    col = power_of_two(jnp.sqrt(jnp.max(diagonal, axis=1, keepdims=True)))
    return (high / row) / col, (low / row) / col, row


def by_weight(products, k, n, m):
    block = lambda i, j: products[i * k : (i + 1) * k, j * k : (j + 1) * k]
    return [sum(block(i, t - i) for i in range(n) if 0 <= t - i < m) for t in range(n + m - 1)]


def factors_kernel(count, g_ref, up_ref, w1_ref, w2_ref, inv2_ref):
    k = g_ref.shape[1]
    high, low, row = scaled(g_ref[0], g_ref[1])
    inv1 = inverse_factor(0.5 * (high + high.T))
    size = power_of_two(jnp.max(jnp.abs(inv1), axis=1, keepdims=True))
    p, left = cut(inv1, size, 3)
    inv1 = inv1 - left
    g, left = cut(high, 1.0, 3)
    g += cut(left + low, 2.0**-24, 2)[0]
    p_rows = jnp.concatenate(p, axis=0)
    y, y_low = descending(by_weight(mm(p_rows, jnp.concatenate(g, axis=1)), k, 3, 5))
    size = power_of_two(jnp.max(jnp.abs(y), axis=1, keepdims=True))
    parts, left = cut(y, size, 3)
    parts += cut(left + y_low, size * 2.0**-24, 1)[0]
    gram2, low = descending(by_weight(mm(jnp.concatenate(parts, axis=0), p_rows, (1, 1)), k, 4, 3))
    r = lax.broadcasted_iota(jnp.int32, (k, k), 0)
    c = lax.broadcasted_iota(jnp.int32, (k, k), 1)
    e = jnp.where(c == r, gram2 - 1.0, gram2) + low
    e = 0.5 * (e + e.T)
    near = jnp.sum(e * e) <= 1.0 / 64.0

    @pl.when(near)
    def _():
        inv2_ref[...] = inverse_factor_near_one(e)

    @pl.when(jnp.logical_not(near))
    def _():
        inv2_ref[...] = inverse_factor(jnp.where(c == r, 1.0 + e, e))

    both = jnp.dot(inv2_ref[...], jnp.concatenate([inv1, y], axis=1), precision=HIGH, preferred_element_type=F32)
    inverse = (both[:, :k] / row) * math.sqrt(count)
    h, m, l = split3(inverse.T)
    hm = jnp.concatenate([h, m], axis=1)
    w1_ref[...] = jnp.concatenate([hm, hm], axis=0)
    w2_ref[...] = jnp.concatenate([l, h], axis=0)
    up_ref[...] = jnp.where(c >= r, (both[:, k:] * row) / math.sqrt(count), 0.0)


def factors(g, count):
    k = g.shape[1]
    return pl.pallas_call(
        lambda *refs: factors_kernel(count, *refs),
        out_shape=(
            jax.ShapeDtypeStruct((k, k), F32),
            jax.ShapeDtypeStruct((2 * k, 2 * k), BF16),
            jax.ShapeDtypeStruct((2 * k, k), BF16),
        ),
        scratch_shapes=[pltpu.VMEM((k, k), F32)],
        compiler_params=pltpu.CompilerParams(vmem_limit_bytes=VMEM_LIMIT),
        name="factors",
    )(g)


def modes_of(rows, w1, w2):
    k = rows.shape[1]
    h, m, l = split3(rows)
    p = mm(jnp.concatenate([h, m], axis=1), w1)
    q = mm(jnp.concatenate([h, l], axis=1), w2)
    return p[:, :k] + (p[:, k:] + q)


def pieces(source, target, sem):
    n = target.shape[0] // 4
    return [
        pltpu.make_async_copy(source.at[pl.ds(i * n, n)], target.at[pl.ds(i * n, n)], sem.at[i]) for i in range(4)
    ]


def chip_kernel(s_ref, chip_ref, w1_ref, w2_ref, modes_hbm, low_ref, mb_ref, modes_ref, put_sem):
    rows = s_ref.shape[0]
    put = pieces(modes_ref, modes_hbm, put_sem)
    per = rows // TILE // 4
    for c in range(4 * per):
        at = slice(c * TILE, (c + 1) * TILE)
        modes = modes_of(s_ref[at, :], w1_ref[...], w2_ref[...])
        modes_ref[at, :] = modes
        mb_ref[0, at, :], low_ref[at, :] = split2(modes)
        if (c + 1) % per == 0:
            put[c // per].start()
    for c in range(4 * per):
        at = slice(c * TILE, (c + 1) * TILE)
        mb_ref[1, at, :] = modes_of(chip_ref[at, :], w1_ref[...], w2_ref[...]).astype(BF16)
    for copy in put:
        copy.wait()


def chip_modes(s, chip, w1, w2):
    rows, k = s.shape
    vmem, hbm = pl.BlockSpec(memory_space=pltpu.VMEM), pl.BlockSpec(memory_space=pl.ANY)
    return pl.pallas_call(
        chip_kernel,
        in_specs=[vmem] * 4,
        out_specs=(hbm, vmem, vmem),
        out_shape=(
            jax.ShapeDtypeStruct((rows, k), F32),
            pltpu.VMEM((rows, k), BF16),
            pltpu.VMEM((2, rows, k), BF16),
        ),
        scratch_shapes=[
            pltpu.VMEM((rows, k), F32),
            pltpu.SemaphoreType.DMA((4,)),
        ],
        compiler_params=pltpu.CompilerParams(vmem_limit_bytes=VMEM_LIMIT),
        name="chip_modes",
    )(in_vmem(s), in_vmem(chip), in_vmem(w1), in_vmem(w2))


def apply_kernel(
    cols_hbm, low_ref, mb_ref, inner_ref, outer_ref, w1_ref, w2_ref, jb_ref, jm_hbm, red_ref,
    all_ref, jm_ref, cols_ref, sem, put_sem,
):
    rows, k = low_ref.shape
    block_rows, slots, blk, _ = jb_ref.shape
    place = lax.axis_index("bulk")
    odd = place % 2
    offsets = (rows, (2 - 2 * odd) * rows, 2 * odd * rows)
    at = [pl.ds(pl.multiple_of(offset, blk), rows) for offset in offsets]
    own = pltpu.make_async_copy(mb_ref.at[0], all_ref.at[at[0]], sem.at[0])
    other = pltpu.make_async_copy(mb_ref.at[1], all_ref.at[at[1]], sem.at[1])
    get_cols = pltpu.make_async_copy(cols_hbm, cols_ref, sem.at[2])
    put = pieces(jm_ref, jm_hbm, put_sem)
    get_cols.start()
    own.start()
    other.start()

    def further(ref):
        for c in range(rows // TILE):
            modes = modes_of(ref[c * TILE : (c + 1) * TILE, :], w1_ref[...], w2_ref[...])
            all_ref[rows_of(c + offsets[2] // TILE, TILE), :] = modes.astype(BF16)

    is_inner = (place % 4 == 1) | (place % 4 == 2)
    pl.when(is_inner)(lambda: further(inner_ref))
    pl.when(jnp.logical_not(is_inner))(lambda: further(outer_ref))
    own.wait()
    other.wait()
    get_cols.wait()
    start = cols_ref[0, 0]

    def apply(r):
        acc = jnp.zeros((blk, k), F32)
        for n in range(0, slots, 2):
            lhs = jnp.concatenate([jb_ref[r, n], jb_ref[r, n + 1]], axis=1)
            picked = []
            for p in (n, n + 1):
                index = cols_ref[r, p] - start + block_rows
                picked.append(all_ref[rows_of(index, blk), :])
            acc = acc + mm(lhs, jnp.concatenate(picked, axis=0))
        jm_ref[rows_of(r, blk), :] = acc.astype(BF16)

    for r in range(block_rows):
        apply(r)
        if (r + 1) % (block_rows // 4) == 0:
            put[r // (block_rows // 4)].start()

    def project(c, acc):
        at = rows_of(c, TILE)
        return acc + mm(jnp.concatenate([mb_ref[0, at, :], low_ref[at, :]], axis=1), jm_ref[at, :], (0, 0))

    acc = lax.fori_loop(0, rows // TILE, project, jnp.zeros((2 * k, k), F32), unroll=True)
    red_ref[...] = acc[:k, :] + acc[k:, :]
    for copy in put:
        copy.wait()


def apply_and_project(cols, low, mb, inner, outer, w1, w2, jb):
    rows, k = low.shape
    vmem, hbm = pl.BlockSpec(memory_space=pltpu.VMEM), pl.BlockSpec(memory_space=pl.ANY)
    return pl.pallas_call(
        apply_kernel,
        in_specs=[hbm] + [vmem] * 7,
        out_specs=(hbm, vmem),
        out_shape=(jax.ShapeDtypeStruct((rows, k), BF16), jax.ShapeDtypeStruct((k, k), F32)),
        scratch_shapes=[
            pltpu.VMEM((3 * rows, k), BF16),
            pltpu.VMEM((rows, k), BF16),
            pltpu.SMEM(cols.shape, jnp.int32),
            pltpu.SemaphoreType.DMA((3,)),
            pltpu.SemaphoreType.DMA((4,)),
        ],
        compiler_params=pltpu.CompilerParams(vmem_limit_bytes=VMEM_LIMIT),
        name="apply_and_project",
    )(cols, in_vmem(low), in_vmem(mb), in_vmem(inner), in_vmem(outer), in_vmem(w1), in_vmem(w2), in_vmem(jb))


def solution(mesh):
    axes = tuple(mesh.axis_names)
    sizes = dict(mesh.shape)
    n_bulk, n_span = sizes["bulk"], sizes["span"]
    count = n_bulk * n_span
    weight = {"bulk": n_span, "span": 1} if axes[0] == "bulk" else {"bulk": 1, "span": n_bulk}
    bits = lambda n: [1 << i for i in range(n.bit_length() - 1)]
    core_mask = weight["bulk"]
    masks = [m * weight["span"] for m in bits(n_span)] + [m * weight["bulk"] for m in bits(n_bulk)[1:]]
    phases = [masks[i : i + 2] for i in range(0, len(masks), 2)]
    masks_x, masks_y = [core_mask * 2], masks[:1]
    others = [m for m in masks if m not in masks_x + masks_y]
    masks_far = [others[i : i + 2] for i in range(0, len(others), 2)]

    def swap(value, mask):
        return lax.ppermute(value, axes, [(i, i ^ mask) for i in range(count)])

    def exchange(value, phase, add):
        if len(phase) == 1:
            return add(value, swap(value, phase[0]))
        a, b = phase
        pa, pb, pab = swap(value, a), swap(value, b), swap(value, a | b)
        return add(add(value, pa), add(pb, pab))

    def shards(snapshots, jac_blocks, jac_cols):
        rows_total = snapshots.shape[0] * count
        even = lax.axis_index("bulk") % 2 == 0
        pairs = lambda first: [p for i in range(first, n_bulk - 1, 4) for p in ((i, i + 1), (i + 1, i))]
        chip = swap(snapshots, core_mask)
        inner = lax.ppermute(snapshots, "bulk", pairs(1))
        gram = local_gram(snapshots)
        half = gram.shape[1] // 2
        upper, lower = gram[:, :half], gram[:, half:]
        mine = add_pairs(jnp.where(even, upper, lower), swap(jnp.where(even, lower, upper), core_mask))
        for phase in masks_far:
            mine = exchange(mine, phase, add_pairs)
        mine, inner = lax.optimization_barrier((mine, inner))
        mine = exchange(mine, masks_x, add_pairs)
        mine, late = lax.optimization_barrier((mine, snapshots))
        outer = lax.ppermute(late, "bulk", pairs(3))
        mine = exchange(mine, masks_y, add_pairs)
        other = swap(mine, core_mask)
        gram = jnp.concatenate([jnp.where(even, mine, other), jnp.where(even, other, mine)], axis=1)
        factor, w1, w2 = factors(gram, rows_total)
        modes, low, mb = chip_modes(snapshots, chip, w1, w2)
        jac_modes, reduced = apply_and_project(jac_cols, low, mb, inner, outer, w1, w2, jac_blocks)
        reduced = reduced + swap(reduced, core_mask)
        for phase in phases:
            reduced = exchange(reduced, phase, jnp.add)
        return modes, factor, jac_modes, reduced / rows_total

    rows = P(("span", "bulk"), None)
    return jax.shard_map(
        shards,
        mesh=mesh,
        in_specs=(rows, P(("span", "bulk"), None, None, None), rows),
        out_specs=(rows, P(), rows, P()),
        check_vma=False,
    )
```

```python
import math

import jax
import jax.numpy as jnp
from jax import lax
from jax.experimental import pallas as pl
from jax.experimental.pallas import tpu as pltpu
from jax.sharding import PartitionSpec as P

F32 = jnp.float32
BF16 = jnp.bfloat16
HIGH = lax.Precision.HIGHEST
VMEM_LIMIT = 24 * 1024 * 1024
CHUNK = 512
TILE = 256


def mm(a, b, contract=(1, 0)):
    return lax.dot_general(a, b, (((contract[0],), (contract[1],)), ((), ())), preferred_element_type=F32)


def split2(x):
    h = x.astype(BF16)
    return h, (x - h.astype(F32)).astype(BF16)


def split3(x):
    h = x.astype(BF16)
    r = x - h.astype(F32)
    m = r.astype(BF16)
    return h, m, (r - m.astype(F32)).astype(BF16)


def in_vmem(x):
    return pltpu.with_memory_space_constraint(x, pltpu.VMEM)


def rows_of(i, n):
    return pl.ds(pl.multiple_of(i * n, n), n)


def two_sum(a, b):
    s = a + b
    t = s - a
    return s, (a - (s - t)) + (b - t)


def descending(terms):
    high, low = terms[0], jnp.zeros_like(terms[0])
    for term in terms[1:]:
        high, error = two_sum(high, term)
        low = low + error
    return high, low


def add_pairs(a, b):
    high, error = two_sum(a[0], b[0])
    low = (a[1] + b[1]) + error
    total = high + low
    return jnp.stack([total, low - (total - high)])


def power_of_two(x):
    q = x * float(2**23 + 1)
    return 2.0 * jnp.abs(q - q * (1.0 - 2.0**-24))


def cut(x, size, n):
    grid = size * (1.5 * 2.0**16)
    parts = []
    for _ in range(n):
        part = (x + grid) - grid
        x = x - part
        parts.append(part.astype(BF16))
        grid = grid * 2.0**-8
    return parts, x


def gram_kernel(s_hbm, g_ref, s_ref, sem):
    rows, k = s_ref.shape
    chunks = rows // CHUNK
    copies = [
        pltpu.make_async_copy(s_hbm.at[pl.ds(c * CHUNK, CHUNK)], s_ref.at[pl.ds(c * CHUNK, CHUNK)], sem.at[c])
        for c in range(chunks)
    ]
    for copy in copies:
        copy.start()
    top = jnp.zeros((8, k), F32)
    for c, copy in enumerate(copies):
        copy.wait()
        rows_here = jnp.abs(s_ref[c * CHUNK : (c + 1) * CHUNK, :])
        top = jnp.maximum(top, jnp.max(rows_here.reshape(CHUNK // 8, 8, k), axis=0))
    size = power_of_two(jnp.max(top, axis=0, keepdims=True))
    zero = jnp.zeros((k, k), F32)
    aa, aa_low, ab, ab_low, odd, even = zero, zero, zero, zero, zero, zero
    for c in range(chunks):
        one, two, three = jnp.zeros((k, 2 * k), F32), jnp.zeros((2 * k, 2 * k), F32), zero
        for at in range(c * CHUNK, (c + 1) * CHUNK, TILE):
            (p, q, r), _ = cut(s_ref[at : at + TILE, :], size, 3)
            pq = jnp.concatenate([p, q], axis=1)
            one = one + mm(p, pq, (0, 0))
            two = two + mm(pq, jnp.concatenate([r, q], axis=1), (0, 0))
            three = three + mm(r, r, (0, 0))
        aa, error = two_sum(aa, one[:, :k])
        aa_low = aa_low + error
        ab, error = two_sum(ab, one[:, k:])
        ab_low = ab_low + error
        odd = odd + (two[:k, :k] + two[k:, :k])
        even = even + (two[k:, k:] + three)
    cross, cross_low = two_sum(ab, ab.T)
    total, total_low = two_sum(aa, cross)
    low = ab_low + (odd + 0.5 * even)
    low = (aa_low + (cross_low + total_low)) + (low + low.T)
    high = total + low
    g_ref[0] = high
    g_ref[1] = low - (high - total)


def local_gram(s):
    rows, k = s.shape
    return pl.pallas_call(
        gram_kernel,
        in_specs=[pl.BlockSpec(memory_space=pl.ANY)],
        out_shape=jax.ShapeDtypeStruct((2, k, k), F32),
        scratch_shapes=[pltpu.VMEM((rows, k), F32), pltpu.SemaphoreType.DMA((rows // CHUNK,))],
        compiler_params=pltpu.CompilerParams(vmem_limit_bytes=VMEM_LIMIT),
        name="local_gram",
    )(s)


def inverse_factor(a):
    k, n = a.shape[0], 8
    blocks = [a[n * i : n * i + n, :] for i in range(k // n)]
    lane = lax.broadcasted_iota(jnp.int32, (n, k), 1)
    sub = lax.broadcasted_iota(jnp.int32, (n, k), 0)
    full = lambda value: jnp.broadcast_to(value, (n, k))
    column_of = lambda x, j: full(x[:, j : j + 1])
    row_of = lambda x, s: full(x[s : s + 1, :])
    below = [(s, t) for t in range(n) for s in range(t, n)]
    first = [column_of(blocks[0], t) for t in range(n)]
    d = {(s, t): row_of(first[t], s) for s, t in below}
    rows = []
    for p in range(k // n):
        at = n * p
        row = [row_of(blocks[p], s) for s in range(n)]
        done, scale, low = [], [], {}
        for t in range(n):
            scale.append(lax.rsqrt(d[t, t]))
            here = lane == at + t
            done.append(jnp.where(here, scale[t], row[t] * scale[t]))
            for s in range(t + 1, n):
                low[s, t] = d[s, t] * scale[t]
            for u in range(t + 1, n):
                for s in range(u, n):
                    d[s, u] = d[s, u] - low[s, t] * low[u, t]
            for s in range(t + 1, n):
                row[s] = jnp.where(here, 0.0, row[s]) - low[s, t] * done[t]
        out = done[0]
        for t in range(1, n):
            out = jnp.where(sub == t, done[t], out)
        rows.append(out)
        panel = (lane >= at) & (lane < at + n)
        terms = [jnp.where(panel & (lane > at + t), 0.0, done[t]) for t in range(n)]
        for i in range(p + 1, k // n):
            x = blocks[i]
            new = jnp.where(panel, 0.0, x)
            column = []
            for t in range(n):
                c = column_of(x, at + t)
                for u in range(t):
                    c = c - column[u] * low[t, u]
                column.append(c * scale[t])
                new = new - column[t] * terms[t]
            blocks[i] = new
            if i == p + 1:
                ahead = [column_of(x, at + n + s) for s in range(n)]
                parts = [[row_of(c, s) for s in range(n)] for c in column]
                for t in range(n - 1):
                    for s in range(n):
                        ahead[s] = ahead[s] - column[t] * parts[t][s]
                last = parts[n - 1]
                d = {(s, t): row_of(ahead[t], s) - last[s] * last[t] for s, t in below}
    x = jnp.concatenate(rows, axis=0)
    r = lax.broadcasted_iota(jnp.int32, (k, k), 0)
    c = lax.broadcasted_iota(jnp.int32, (k, k), 1)
    return jnp.where(c <= r, x, 0.0)


def mm3(a, b, contract=(1, 0)):
    ah, am = split2(a)
    bh, bm = split2(b)
    return mm(ah, bh, contract) + (mm(ah, bm, contract) + mm(am, bh, contract))


def inverse_factor_near_one(e):
    k = e.shape[0]
    r = lax.broadcasted_iota(jnp.int32, (k, k), 0)
    c = lax.broadcasted_iota(jnp.int32, (k, k), 1)
    half = lambda x: jnp.where(c < r, x, jnp.where(c == r, 0.5 * x, 0.0))
    f = half(e)
    ff = mm3(f, f)
    n = half(mm3(f, f, (1, 1)) + (ff + ff.T)) - f
    ne = mm3(n, e)
    left = (e + (n + n.T)) + ((ne + ne.T) + mm3(n + ne, n, (1, 1)))
    step = half(left)
    return jnp.where(c == r, 1.0, 0.0) + (n - (step + mm3(step, n)))


def scaled(high, low):
    k = high.shape[0]
    r = lax.broadcasted_iota(jnp.int32, (k, k), 0)
    c = lax.broadcasted_iota(jnp.int32, (k, k), 1)
    diagonal = jnp.where(r == c, high, 0.0)
    row = power_of_two(jnp.sqrt(jnp.max(diagonal, axis=0, keepdims=True)))
    col = power_of_two(jnp.sqrt(jnp.max(diagonal, axis=1, keepdims=True)))
    return (high / row) / col, (low / row) / col, row


def by_weight(products, k, n, m):
    block = lambda i, j: products[i * k : (i + 1) * k, j * k : (j + 1) * k]
    return [sum(block(i, t - i) for i in range(n) if 0 <= t - i < m) for t in range(n + m - 1)]


def modes_of(rows, w1, w2):
    k = rows.shape[1]
    h, m, l = split3(rows)
    p = mm(jnp.concatenate([h, m], axis=1), w1)
    q = mm(jnp.concatenate([h, l], axis=1), w2)
    return p[:, :k] + (p[:, k:] + q)


def factors_kernel(count, g_ref, s_ref, chip_ref, up_ref, w1_ref, w2_ref, modes_ref, low_ref, mb_ref, inv2_ref):
    k = g_ref.shape[1]
    high, low, row = scaled(g_ref[0], g_ref[1])
    inv1 = inverse_factor(0.5 * (high + high.T))
    size = power_of_two(jnp.max(jnp.abs(inv1), axis=1, keepdims=True))
    p, left = cut(inv1, size, 3)
    inv1 = inv1 - left
    g, left = cut(high, 1.0, 3)
    g += cut(left + low, 2.0**-24, 2)[0]
    p_rows = jnp.concatenate(p, axis=0)
    y, y_low = descending(by_weight(mm(p_rows, jnp.concatenate(g, axis=1)), k, 3, 5))
    size = power_of_two(jnp.max(jnp.abs(y), axis=1, keepdims=True))
    parts, left = cut(y, size, 3)
    parts += cut(left + y_low, size * 2.0**-24, 1)[0]
    gram2, low = descending(by_weight(mm(jnp.concatenate(parts, axis=0), p_rows, (1, 1)), k, 4, 3))
    r = lax.broadcasted_iota(jnp.int32, (k, k), 0)
    c = lax.broadcasted_iota(jnp.int32, (k, k), 1)
    e = jnp.where(c == r, gram2 - 1.0, gram2) + low
    e = 0.5 * (e + e.T)
    near = jnp.sum(e * e) <= 1.0 / 64.0

    @pl.when(near)
    def _():
        inv2_ref[...] = inverse_factor_near_one(e)

    @pl.when(jnp.logical_not(near))
    def _():
        inv2_ref[...] = inverse_factor(jnp.where(c == r, 1.0 + e, e))

    both = jnp.dot(inv2_ref[...], jnp.concatenate([inv1, y], axis=1), precision=HIGH, preferred_element_type=F32)
    inverse = (both[:, :k] / row) * math.sqrt(count)
    h, m, l = split3(inverse.T)
    hm = jnp.concatenate([h, m], axis=1)
    w1_ref[...] = jnp.concatenate([hm, hm], axis=0)
    w2_ref[...] = jnp.concatenate([l, h], axis=0)
    up_ref[...] = jnp.where(c >= r, (both[:, k:] * row) / math.sqrt(count), 0.0)
    for at in (slice(i, i + TILE) for i in range(0, s_ref.shape[0], TILE)):
        modes = modes_of(s_ref[at, :], w1_ref[...], w2_ref[...])
        modes_ref[at, :] = modes
        mb_ref[0, at, :], low_ref[at, :] = split2(modes)
    for at in (slice(i, i + TILE) for i in range(0, s_ref.shape[0], TILE)):
        mb_ref[1, at, :] = modes_of(chip_ref[at, :], w1_ref[...], w2_ref[...]).astype(BF16)


def factors_and_chip_modes(g, s, chip, count):
    rows, k = s.shape
    vmem = pl.BlockSpec(memory_space=pltpu.VMEM)
    return pl.pallas_call(
        lambda *refs: factors_kernel(count, *refs),
        in_specs=[vmem] * 3,
        out_specs=(vmem,) * 6,
        out_shape=(
            jax.ShapeDtypeStruct((k, k), F32),
            pltpu.VMEM((2 * k, 2 * k), BF16),
            pltpu.VMEM((2 * k, k), BF16),
            pltpu.VMEM((rows, k), F32),
            pltpu.VMEM((rows, k), BF16),
            pltpu.VMEM((2, rows, k), BF16),
        ),
        scratch_shapes=[pltpu.VMEM((k, k), F32)],
        compiler_params=pltpu.CompilerParams(vmem_limit_bytes=VMEM_LIMIT),
        name="factors_and_chip_modes",
    )(in_vmem(g), in_vmem(s), in_vmem(chip))


def apply_kernel(
    cols_hbm, modes_ref, low_ref, mb_ref, inner_ref, outer_ref, w1_ref, w2_ref, jb_ref, modes_hbm, jm_ref, red_ref,
    all_ref, cols_ref, sem,
):
    rows, k = low_ref.shape
    block_rows, slots, blk, _ = jb_ref.shape
    place = lax.axis_index("bulk")
    odd = place % 2
    offsets = (rows, (2 - 2 * odd) * rows, 2 * odd * rows)
    at = [pl.ds(pl.multiple_of(offset, blk), rows) for offset in offsets]
    own = pltpu.make_async_copy(mb_ref.at[0], all_ref.at[at[0]], sem.at[0])
    other = pltpu.make_async_copy(mb_ref.at[1], all_ref.at[at[1]], sem.at[1])
    get_cols = pltpu.make_async_copy(cols_hbm, cols_ref, sem.at[2])
    put_modes = pltpu.make_async_copy(modes_ref, modes_hbm, sem.at[3])
    get_cols.start()
    own.start()
    other.start()
    put_modes.start()

    def further(ref):
        for c in range(rows // TILE):
            modes = modes_of(ref[c * TILE : (c + 1) * TILE, :], w1_ref[...], w2_ref[...])
            all_ref[rows_of(c + offsets[2] // TILE, TILE), :] = modes.astype(BF16)

    is_inner = (place % 4 == 1) | (place % 4 == 2)
    pl.when(is_inner)(lambda: further(inner_ref))
    pl.when(jnp.logical_not(is_inner))(lambda: further(outer_ref))
    own.wait()
    other.wait()
    get_cols.wait()
    start = cols_ref[0, 0]

    def apply(r):
        acc = jnp.zeros((blk, k), F32)
        for n in range(0, slots, 2):
            lhs = jnp.concatenate([jb_ref[r, n], jb_ref[r, n + 1]], axis=1)
            picked = []
            for p in (n, n + 1):
                index = cols_ref[r, p] - start + block_rows
                picked.append(all_ref[rows_of(index, blk), :])
            acc = acc + mm(lhs, jnp.concatenate(picked, axis=0))
        jm_ref[rows_of(r, blk), :] = acc.astype(BF16)

    for r in range(block_rows):
        apply(r)

    def project(c, acc):
        at = rows_of(c, TILE)
        return acc + mm(jnp.concatenate([mb_ref[0, at, :], low_ref[at, :]], axis=1), jm_ref[at, :], (0, 0))

    acc = lax.fori_loop(0, rows // TILE, project, jnp.zeros((2 * k, k), F32), unroll=True)
    red_ref[...] = acc[:k, :] + acc[k:, :]
    put_modes.wait()


def apply_and_project(cols, modes, low, mb, inner, outer, w1, w2, jb):
    rows, k = low.shape
    vmem, hbm = pl.BlockSpec(memory_space=pltpu.VMEM), pl.BlockSpec(memory_space=pl.ANY)
    return pl.pallas_call(
        apply_kernel,
        in_specs=[hbm] + [vmem] * 8,
        out_specs=(hbm, vmem, vmem),
        out_shape=(
            jax.ShapeDtypeStruct((rows, k), F32),
            pltpu.VMEM((rows, k), BF16),
            pltpu.VMEM((k, k), F32),
        ),
        scratch_shapes=[
            pltpu.VMEM((3 * rows, k), BF16),
            pltpu.SMEM(cols.shape, jnp.int32),
            pltpu.SemaphoreType.DMA((4,)),
        ],
        compiler_params=pltpu.CompilerParams(vmem_limit_bytes=VMEM_LIMIT),
        name="apply_and_project",
    )(cols, in_vmem(modes), in_vmem(low), in_vmem(mb), in_vmem(inner), in_vmem(outer), in_vmem(w1), in_vmem(w2), in_vmem(jb))


def solution(mesh):
    axes = tuple(mesh.axis_names)
    sizes = dict(mesh.shape)
    n_bulk, n_span = sizes["bulk"], sizes["span"]
    count = n_bulk * n_span
    weight = {"bulk": n_span, "span": 1} if axes[0] == "bulk" else {"bulk": 1, "span": n_bulk}
    bits = lambda n: [1 << i for i in range(n.bit_length() - 1)]
    core_mask = weight["bulk"]
    masks = [m * weight["span"] for m in bits(n_span)] + [m * weight["bulk"] for m in bits(n_bulk)[1:]]
    phases = [masks[i : i + 2] for i in range(0, len(masks), 2)]
    masks_x, masks_y = [core_mask * 2], masks[:1]
    others = [m for m in masks if m not in masks_x + masks_y]
    masks_far = [others[i : i + 2] for i in range(0, len(others), 2)]

    def swap(value, mask):
        return lax.ppermute(value, axes, [(i, i ^ mask) for i in range(count)])

    def exchange(value, phase, add):
        if len(phase) == 1:
            return add(value, swap(value, phase[0]))
        a, b = phase
        pa, pb, pab = swap(value, a), swap(value, b), swap(value, a | b)
        return add(add(value, pa), add(pb, pab))

    def shards(snapshots, jac_blocks, jac_cols):
        rows_total = snapshots.shape[0] * count
        even = lax.axis_index("bulk") % 2 == 0
        pairs = lambda first: [p for i in range(first, n_bulk - 1, 4) for p in ((i, i + 1), (i + 1, i))]
        chip = swap(snapshots, core_mask)
        inner = lax.ppermute(snapshots, "bulk", pairs(1))
        gram = local_gram(snapshots)
        half = gram.shape[1] // 2
        upper, lower = gram[:, :half], gram[:, half:]
        mine = add_pairs(jnp.where(even, upper, lower), swap(jnp.where(even, lower, upper), core_mask))
        for phase in masks_far:
            mine = exchange(mine, phase, add_pairs)
        mine, inner, late = lax.optimization_barrier((mine, inner, snapshots))
        mine = exchange(mine, masks_x, add_pairs)
        outer = lax.ppermute(late, "bulk", pairs(3))
        mine = exchange(mine, masks_y, add_pairs)
        other = swap(mine, core_mask)
        gram = jnp.concatenate([jnp.where(even, mine, other), jnp.where(even, other, mine)], axis=1)
        factor, w1, w2, modes, low, mb = factors_and_chip_modes(gram, snapshots, chip, rows_total)
        modes, jac_modes, reduced = apply_and_project(jac_cols, modes, low, mb, inner, outer, w1, w2, jac_blocks)
        reduced = reduced + swap(reduced, core_mask)
        for phase in phases:
            reduced = exchange(reduced, phase, jnp.add)
        return modes, factor, jac_modes, reduced / rows_total

    rows = P(("span", "bulk"), None)
    return jax.shard_map(
        shards,
        mesh=mesh,
        in_specs=(rows, P(("span", "bulk"), None, None, None), rows),
        out_specs=(rows, P(), rows, P()),
        check_vma=False,
    )
```

```python
import math

import jax
import jax.numpy as jnp
from jax import lax
from jax.experimental import pallas as pl
from jax.experimental.pallas import tpu as pltpu
from jax.sharding import PartitionSpec as P

F32 = jnp.float32
BF16 = jnp.bfloat16
VMEM_LIMIT = 24 * 1024 * 1024
CHUNK = 512
TILE = 256


def mm(a, b, contract=(1, 0)):
    return lax.dot_general(a, b, (((contract[0],), (contract[1],)), ((), ())), preferred_element_type=F32)


def split2(x):
    h = x.astype(BF16)
    return h, (x - h.astype(F32)).astype(BF16)


def split3(x):
    h = x.astype(BF16)
    r = x - h.astype(F32)
    m = r.astype(BF16)
    return h, m, (r - m.astype(F32)).astype(BF16)


def in_vmem(x):
    return pltpu.with_memory_space_constraint(x, pltpu.VMEM)


def rows_of(i, n):
    return pl.ds(pl.multiple_of(i * n, n), n)


def two_sum(a, b):
    s = a + b
    t = s - a
    return s, (a - (s - t)) + (b - t)


def descending(terms):
    high, low = terms[0], jnp.zeros_like(terms[0])
    for term in terms[1:]:
        high, error = two_sum(high, term)
        low = low + error
    return high, low


def add_pairs(a, b):
    high, error = two_sum(a[0], b[0])
    low = (a[1] + b[1]) + error
    total = high + low
    return jnp.stack([total, low - (total - high)])


def power_of_two(x):
    q = x * float(2**23 + 1)
    return 2.0 * jnp.abs(q - q * (1.0 - 2.0**-24))


def cut(x, size, n):
    grid = size * (1.5 * 2.0**16)
    parts = []
    for _ in range(n):
        part = (x + grid) - grid
        x = x - part
        parts.append(part.astype(BF16))
        grid = grid * 2.0**-8
    return parts, x


def gram_kernel(s_hbm, g_ref, s_ref, sem):
    rows, k = s_ref.shape
    chunks = rows // CHUNK
    copies = [
        pltpu.make_async_copy(s_hbm.at[pl.ds(c * CHUNK, CHUNK)], s_ref.at[pl.ds(c * CHUNK, CHUNK)], sem.at[c])
        for c in range(chunks)
    ]
    for copy in copies:
        copy.start()
    top = jnp.zeros((8, k), F32)
    for c, copy in enumerate(copies):
        copy.wait()
        rows_here = jnp.abs(s_ref[c * CHUNK : (c + 1) * CHUNK, :])
        top = jnp.maximum(top, jnp.max(rows_here.reshape(CHUNK // 8, 8, k), axis=0))
    size = power_of_two(jnp.max(top, axis=0, keepdims=True))
    zero = jnp.zeros((k, k), F32)
    aa, aa_low, ab, ab_low, odd, even = zero, zero, zero, zero, zero, zero
    for c in range(chunks):
        one, two, three = jnp.zeros((k, 2 * k), F32), jnp.zeros((2 * k, 2 * k), F32), zero
        for at in range(c * CHUNK, (c + 1) * CHUNK, TILE):
            (p, q, r), _ = cut(s_ref[at : at + TILE, :], size, 3)
            pq = jnp.concatenate([p, q], axis=1)
            one = one + mm(p, pq, (0, 0))
            two = two + mm(pq, jnp.concatenate([r, q], axis=1), (0, 0))
            three = three + mm(r, r, (0, 0))
        aa, error = two_sum(aa, one[:, :k])
        aa_low = aa_low + error
        ab, error = two_sum(ab, one[:, k:])
        ab_low = ab_low + error
        odd = odd + (two[:k, :k] + two[k:, :k])
        even = even + (two[k:, k:] + three)
    cross, cross_low = two_sum(ab, ab.T)
    total, total_low = two_sum(aa, cross)
    low = ab_low + (odd + 0.5 * even)
    low = (aa_low + (cross_low + total_low)) + (low + low.T)
    high = total + low
    g_ref[0] = high
    g_ref[1] = low - (high - total)


def local_gram(s):
    rows, k = s.shape
    return pl.pallas_call(
        gram_kernel,
        in_specs=[pl.BlockSpec(memory_space=pl.ANY)],
        out_shape=jax.ShapeDtypeStruct((2, k, k), F32),
        scratch_shapes=[pltpu.VMEM((rows, k), F32), pltpu.SemaphoreType.DMA((rows // CHUNK,))],
        compiler_params=pltpu.CompilerParams(vmem_limit_bytes=VMEM_LIMIT),
        name="local_gram",
    )(s)


def inverse_factor(a):
    k, n = a.shape[0], 8
    blocks = [a[n * i : n * i + n, :] for i in range(k // n)]
    lane = lax.broadcasted_iota(jnp.int32, (n, k), 1)
    sub = lax.broadcasted_iota(jnp.int32, (n, k), 0)
    full = lambda value: jnp.broadcast_to(value, (n, k))
    column_of = lambda x, j: full(x[:, j : j + 1])
    row_of = lambda x, s: full(x[s : s + 1, :])
    below = [(s, t) for t in range(n) for s in range(t, n)]
    first = [column_of(blocks[0], t) for t in range(n)]
    d = {(s, t): row_of(first[t], s) for s, t in below}
    rows = []
    for p in range(k // n):
        at = n * p
        row = [row_of(blocks[p], s) for s in range(n)]
        done, scale, low = [], [], {}
        for t in range(n):
            scale.append(lax.rsqrt(d[t, t]))
            here = lane == at + t
            done.append(jnp.where(here, scale[t], row[t] * scale[t]))
            for s in range(t + 1, n):
                low[s, t] = d[s, t] * scale[t]
            for u in range(t + 1, n):
                for s in range(u, n):
                    d[s, u] = d[s, u] - low[s, t] * low[u, t]
            for s in range(t + 1, n):
                row[s] = jnp.where(here, 0.0, row[s]) - low[s, t] * done[t]
        out = done[0]
        for t in range(1, n):
            out = jnp.where(sub == t, done[t], out)
        rows.append(out)
        panel = (lane >= at) & (lane < at + n)
        terms = [jnp.where(panel & (lane > at + t), 0.0, done[t]) for t in range(n)]
        for i in range(p + 1, k // n):
            x = blocks[i]
            new = jnp.where(panel, 0.0, x)
            column = []
            for t in range(n):
                c = column_of(x, at + t)
                for u in range(t):
                    c = c - column[u] * low[t, u]
                column.append(c * scale[t])
                new = new - column[t] * terms[t]
            blocks[i] = new
            if i == p + 1:
                ahead = [column_of(x, at + n + s) for s in range(n)]
                parts = [[row_of(c, s) for s in range(n)] for c in column]
                for t in range(n - 1):
                    for s in range(n):
                        ahead[s] = ahead[s] - column[t] * parts[t][s]
                last = parts[n - 1]
                d = {(s, t): row_of(ahead[t], s) - last[s] * last[t] for s, t in below}
    x = jnp.concatenate(rows, axis=0)
    r = lax.broadcasted_iota(jnp.int32, (k, k), 0)
    c = lax.broadcasted_iota(jnp.int32, (k, k), 1)
    return jnp.where(c <= r, x, 0.0)


def mm3(a, b, contract=(1, 0)):
    ah, am = split2(a)
    bh, bm = split2(b)
    return mm(ah, bh, contract) + (mm(ah, bm, contract) + mm(am, bh, contract))


def inverse_factor_near_one(e):
    k = e.shape[0]
    r = lax.broadcasted_iota(jnp.int32, (k, k), 0)
    c = lax.broadcasted_iota(jnp.int32, (k, k), 1)
    half = lambda x: jnp.where(c < r, x, jnp.where(c == r, 0.5 * x, 0.0))
    f = half(e)
    fb = f.astype(BF16)
    ff = mm(fb, fb)
    n = half(mm(fb, fb, (1, 1)) + (ff + ff.T)) - f
    ne = mm3(n, e)
    left = (e + (n + n.T)) + ((ne + ne.T) + mm3(n + ne, n, (1, 1)))
    step = half(left)
    return n - (step + mm(step.astype(BF16), n.astype(BF16)))


def scaled(high, low):
    k = high.shape[0]
    r = lax.broadcasted_iota(jnp.int32, (k, k), 0)
    c = lax.broadcasted_iota(jnp.int32, (k, k), 1)
    diagonal = jnp.where(r == c, high, 0.0)
    row = power_of_two(jnp.sqrt(jnp.max(diagonal, axis=0, keepdims=True)))
    col = power_of_two(jnp.sqrt(jnp.max(diagonal, axis=1, keepdims=True)))
    inv_row, inv_col = 1.0 / row, 1.0 / col
    return (high * inv_row) * inv_col, (low * inv_row) * inv_col, row, inv_row


def by_weight(products, k, n, m):
    block = lambda i, j: products[i * k : (i + 1) * k, j * k : (j + 1) * k]
    return [sum(block(i, t - i) for i in range(n) if 0 <= t - i < m) for t in range(n + m - 1)]


def modes_of(rows, w1, w2):
    k = rows.shape[1]
    h, m, l = split3(rows)
    p = mm(jnp.concatenate([h, m], axis=1), w1)
    q = mm(jnp.concatenate([h, l], axis=1), w2)
    return p[:, :k] + (p[:, k:] + q)


def factors_kernel(count, g_ref, s_ref, chip_ref, up_ref, w1_ref, w2_ref, modes_ref, low_ref, mb_ref, more_ref):
    k = g_ref.shape[1]
    high, low, row, inv_row = scaled(g_ref[0], g_ref[1])
    inv1 = inverse_factor(high)
    size = power_of_two(jnp.max(jnp.abs(inv1), axis=1, keepdims=True))
    p, left = cut(inv1, size, 3)
    inv1 = inv1 - left
    g, left = cut(high, 1.0, 3)
    g += cut(left + low, 2.0**-24, 2)[0]
    p_rows = jnp.concatenate(p, axis=0)
    y, y_low = descending(by_weight(mm(p_rows, jnp.concatenate(g, axis=1)), k, 3, 5))
    size = power_of_two(jnp.max(jnp.abs(y), axis=1, keepdims=True))
    parts, left = cut(y, size, 3)
    parts += cut(left + y_low, size * 2.0**-24, 1)[0]
    gram2, low = descending(by_weight(mm(jnp.concatenate(parts, axis=0), p_rows, (1, 1)), k, 4, 3))
    r = lax.broadcasted_iota(jnp.int32, (k, k), 0)
    c = lax.broadcasted_iota(jnp.int32, (k, k), 1)
    e = jnp.where(c == r, gram2 - 1.0, gram2) + low
    e = 0.5 * (e + e.T)
    near = jnp.sum(e * e) <= 1.0 / 64.0

    @pl.when(near)
    def _():
        more_ref[...] = inverse_factor_near_one(e)

    @pl.when(jnp.logical_not(near))
    def _():
        inv2 = inverse_factor(jnp.where(c == r, 1.0 + e, e))
        more_ref[...] = jnp.where(c == r, inv2 - 1.0, inv2)

    both = jnp.concatenate([inv1, y], axis=1)
    both = both + mm3(more_ref[...], both)
    inverse = (both[:, :k] * inv_row) * math.sqrt(count)
    h, m, l = split3(inverse.T)
    hm = jnp.concatenate([h, m], axis=1)
    w1_ref[...] = jnp.concatenate([hm, hm], axis=0)
    w2_ref[...] = jnp.concatenate([l, h], axis=0)
    up_ref[...] = jnp.where(c >= r, (both[:, k:] * row) * (1.0 / math.sqrt(count)), 0.0)
    for at in (slice(i, i + TILE) for i in range(0, s_ref.shape[0], TILE)):
        modes = modes_of(s_ref[at, :], w1_ref[...], w2_ref[...])
        modes_ref[at, :] = modes
        mb_ref[0, at, :], low_ref[at, :] = split2(modes)
    for at in (slice(i, i + TILE) for i in range(0, s_ref.shape[0], TILE)):
        mb_ref[1, at, :] = modes_of(chip_ref[at, :], w1_ref[...], w2_ref[...]).astype(BF16)


def factors_and_chip_modes(g, s, chip, count):
    rows, k = s.shape
    vmem = pl.BlockSpec(memory_space=pltpu.VMEM)
    return pl.pallas_call(
        lambda *refs: factors_kernel(count, *refs),
        in_specs=[vmem] * 3,
        out_specs=(vmem,) * 6,
        out_shape=(
            jax.ShapeDtypeStruct((k, k), F32),
            pltpu.VMEM((2 * k, 2 * k), BF16),
            pltpu.VMEM((2 * k, k), BF16),
            pltpu.VMEM((rows, k), F32),
            pltpu.VMEM((rows, k), BF16),
            pltpu.VMEM((2, rows, k), BF16),
        ),
        scratch_shapes=[pltpu.VMEM((k, k), F32)],
        compiler_params=pltpu.CompilerParams(vmem_limit_bytes=VMEM_LIMIT),
        name="factors_and_chip_modes",
    )(in_vmem(g), in_vmem(s), in_vmem(chip))


def apply_kernel(
    cols_hbm, modes_ref, low_ref, mb_ref, inner_ref, outer_ref, w1_ref, w2_ref, jb_ref, modes_hbm, jm_ref, red_ref,
    all_ref, cols_ref, sem,
):
    rows, k = low_ref.shape
    block_rows, slots, blk, _ = jb_ref.shape
    place = lax.axis_index("bulk")
    odd = place % 2
    offsets = (rows, (2 - 2 * odd) * rows, 2 * odd * rows)
    at = [pl.ds(pl.multiple_of(offset, blk), rows) for offset in offsets]
    own = pltpu.make_async_copy(mb_ref.at[0], all_ref.at[at[0]], sem.at[0])
    other = pltpu.make_async_copy(mb_ref.at[1], all_ref.at[at[1]], sem.at[1])
    get_cols = pltpu.make_async_copy(cols_hbm, cols_ref, sem.at[2])
    put_modes = pltpu.make_async_copy(modes_ref, modes_hbm, sem.at[3])
    get_cols.start()
    own.start()
    other.start()
    put_modes.start()

    def further(ref):
        for c in range(rows // TILE):
            modes = modes_of(ref[c * TILE : (c + 1) * TILE, :], w1_ref[...], w2_ref[...])
            all_ref[rows_of(c + offsets[2] // TILE, TILE), :] = modes.astype(BF16)

    is_inner = (place % 4 == 1) | (place % 4 == 2)
    pl.when(is_inner)(lambda: further(inner_ref))
    pl.when(jnp.logical_not(is_inner))(lambda: further(outer_ref))
    own.wait()
    other.wait()
    get_cols.wait()
    start = cols_ref[0, 0]

    def apply(r):
        acc = jnp.zeros((blk, k), F32)
        for n in range(0, slots, 2):
            lhs = jnp.concatenate([jb_ref[r, n], jb_ref[r, n + 1]], axis=1)
            picked = []
            for p in (n, n + 1):
                index = cols_ref[r, p] - start + block_rows
                picked.append(all_ref[rows_of(index, blk), :])
            acc = acc + mm(lhs, jnp.concatenate(picked, axis=0))
        jm_ref[rows_of(r, blk), :] = acc.astype(BF16)

    for r in range(block_rows):
        apply(r)

    def project(c, acc):
        at = rows_of(c, TILE)
        return acc + mm(jnp.concatenate([mb_ref[0, at, :], low_ref[at, :]], axis=1), jm_ref[at, :], (0, 0))

    acc = lax.fori_loop(0, rows // TILE, project, jnp.zeros((2 * k, k), F32), unroll=True)
    red_ref[...] = acc[:k, :] + acc[k:, :]
    put_modes.wait()


def apply_and_project(cols, modes, low, mb, inner, outer, w1, w2, jb):
    rows, k = low.shape
    vmem, hbm = pl.BlockSpec(memory_space=pltpu.VMEM), pl.BlockSpec(memory_space=pl.ANY)
    return pl.pallas_call(
        apply_kernel,
        in_specs=[hbm] + [vmem] * 8,
        out_specs=(hbm, vmem, vmem),
        out_shape=(
            jax.ShapeDtypeStruct((rows, k), F32),
            pltpu.VMEM((rows, k), BF16),
            pltpu.VMEM((k, k), F32),
        ),
        scratch_shapes=[
            pltpu.VMEM((3 * rows, k), BF16),
            pltpu.SMEM(cols.shape, jnp.int32),
            pltpu.SemaphoreType.DMA((4,)),
        ],
        compiler_params=pltpu.CompilerParams(vmem_limit_bytes=VMEM_LIMIT),
        name="apply_and_project",
    )(cols, in_vmem(modes), in_vmem(low), in_vmem(mb), in_vmem(inner), in_vmem(outer), in_vmem(w1), in_vmem(w2), in_vmem(jb))


def solution(mesh):
    axes = tuple(mesh.axis_names)
    sizes = dict(mesh.shape)
    n_bulk, n_span = sizes["bulk"], sizes["span"]
    count = n_bulk * n_span
    weight = {"bulk": n_span, "span": 1} if axes[0] == "bulk" else {"bulk": 1, "span": n_bulk}
    bits = lambda n: [1 << i for i in range(n.bit_length() - 1)]
    core_mask = weight["bulk"]
    masks = [m * weight["span"] for m in bits(n_span)] + [m * weight["bulk"] for m in bits(n_bulk)[1:]]
    phases = [masks[i : i + 2] for i in range(0, len(masks), 2)]
    masks_x, masks_y = [core_mask * 2], masks[:1]
    others = [m for m in masks if m not in masks_x + masks_y]
    masks_far = [others[i : i + 2] for i in range(0, len(others), 2)]

    def swap(value, mask):
        return lax.ppermute(value, axes, [(i, i ^ mask) for i in range(count)])

    def exchange(value, phase, add):
        if len(phase) == 1:
            return add(value, swap(value, phase[0]))
        a, b = phase
        pa, pb, pab = swap(value, a), swap(value, b), swap(value, a | b)
        return add(add(value, pa), add(pb, pab))

    def shards(snapshots, jac_blocks, jac_cols):
        rows_total = snapshots.shape[0] * count
        even = lax.axis_index("bulk") % 2 == 0
        pairs = lambda first: [p for i in range(first, n_bulk - 1, 4) for p in ((i, i + 1), (i + 1, i))]
        chip = swap(snapshots, core_mask)
        inner = lax.ppermute(snapshots, "bulk", pairs(1))
        gram = local_gram(snapshots)
        half = gram.shape[1] // 2
        upper, lower = gram[:, :half], gram[:, half:]
        mine = add_pairs(jnp.where(even, upper, lower), swap(jnp.where(even, lower, upper), core_mask))
        mine, chip = lax.optimization_barrier((mine, chip))
        for phase in masks_far:
            mine = exchange(mine, phase, add_pairs)
        mine, inner, late = lax.optimization_barrier((mine, inner, snapshots))
        mine = exchange(mine, masks_x, add_pairs)
        outer = lax.ppermute(late, "bulk", pairs(3))
        along_y, other, across = (swap(mine, mask) for mask in (masks_y[0], core_mask, masks_y[0] | core_mask))
        mine, other = add_pairs(mine, along_y), add_pairs(other, across)
        gram = jnp.concatenate([jnp.where(even, mine, other), jnp.where(even, other, mine)], axis=1)
        factor, w1, w2, modes, low, mb = factors_and_chip_modes(gram, snapshots, chip, rows_total)
        modes, jac_modes, reduced = apply_and_project(jac_cols, modes, low, mb, inner, outer, w1, w2, jac_blocks)
        reduced = reduced + swap(reduced, core_mask)
        for phase in phases:
            reduced = exchange(reduced, phase, jnp.add)
        return modes, factor, jac_modes, reduced / rows_total

    rows = P(("span", "bulk"), None)
    return jax.shard_map(
        shards,
        mesh=mesh,
        in_specs=(rows, P(("span", "bulk"), None, None, None), rows),
        out_specs=(rows, P(), rows, P()),
        check_vma=False,
    )
```

```python
import math

import jax
import jax.numpy as jnp
from jax import lax
from jax.experimental import pallas as pl
from jax.experimental.pallas import tpu as pltpu
from jax.sharding import PartitionSpec as P

F32 = jnp.float32
BF16 = jnp.bfloat16
VMEM_LIMIT = 24 * 1024 * 1024
CHUNK = 512
TILE = 256


def mm(a, b, contract=(1, 0)):
    return lax.dot_general(a, b, (((contract[0],), (contract[1],)), ((), ())), preferred_element_type=F32)


def split2(x):
    h = x.astype(BF16)
    return h, (x - h.astype(F32)).astype(BF16)


def split3(x):
    h = x.astype(BF16)
    r = x - h.astype(F32)
    m = r.astype(BF16)
    return h, m, (r - m.astype(F32)).astype(BF16)


def in_vmem(x):
    return pltpu.with_memory_space_constraint(x, pltpu.VMEM)


def rows_of(i, n):
    return pl.ds(pl.multiple_of(i * n, n), n)


def two_sum(a, b):
    s = a + b
    t = s - a
    return s, (a - (s - t)) + (b - t)


def descending(terms):
    high, low = terms[0], jnp.zeros_like(terms[0])
    for term in terms[1:]:
        high, error = two_sum(high, term)
        low = low + error
    return high, low


def add_pairs(a, b):
    high, error = two_sum(a[0], b[0])
    low = (a[1] + b[1]) + error
    total = high + low
    return jnp.stack([total, low - (total - high)])


def power_of_two(x):
    q = x * float(2**23 + 1)
    return 2.0 * jnp.abs(q - q * (1.0 - 2.0**-24))


def cut(x, size, n):
    grid = size * (1.5 * 2.0**16)
    parts = []
    for _ in range(n):
        part = (x + grid) - grid
        x = x - part
        parts.append(part.astype(BF16))
        grid = grid * 2.0**-8
    return parts, x


def packed(x):
    k, n = x.shape[0], 8
    lane = lax.broadcasted_iota(jnp.int32, (n, k), 1)
    count = k // n
    block = lambda b: x[n * b : n * b + n, :]
    rows = [block(0)]
    for b in range(1, count // 2):
        rows.append(jnp.where(lane >= n * b, block(b), pltpu.roll(block(count - b), n * b, 1)))
    return jnp.concatenate(rows + [block(count // 2)] * 2, axis=0)


def unpacked(x):
    k, n = x.shape[1], 8
    count = k // n
    block = lambda b: x[n * b : n * b + n, :]
    rows = [block(b) for b in range(count // 2 + 1)]
    rows += [pltpu.roll(block(count - b), k - n * (count - b), 1) for b in range(count // 2 + 1, count)]
    x = jnp.concatenate(rows, axis=0)
    r = lax.broadcasted_iota(jnp.int32, (k, k), 0)
    c = lax.broadcasted_iota(jnp.int32, (k, k), 1)
    return jnp.where((c >> 3) >= (r >> 3), x, x.T)


def gram_kernel(s_hbm, g_ref, s_ref, sem):
    rows, k = s_ref.shape
    chunks = rows // CHUNK
    copies = [
        pltpu.make_async_copy(s_hbm.at[pl.ds(c * CHUNK, CHUNK)], s_ref.at[pl.ds(c * CHUNK, CHUNK)], sem.at[c])
        for c in range(chunks)
    ]
    for copy in copies:
        copy.start()
    top = jnp.zeros((8, k), F32)
    for c, copy in enumerate(copies):
        copy.wait()
        rows_here = jnp.abs(s_ref[c * CHUNK : (c + 1) * CHUNK, :])
        top = jnp.maximum(top, jnp.max(rows_here.reshape(CHUNK // 8, 8, k), axis=0))
    size = power_of_two(jnp.max(top, axis=0, keepdims=True))
    zero = jnp.zeros((k, k), F32)
    aa, aa_low, ab, ab_low, odd, even = zero, zero, zero, zero, zero, zero
    for c in range(chunks):
        one, two, three = jnp.zeros((k, 2 * k), F32), jnp.zeros((2 * k, 2 * k), F32), zero
        for at in range(c * CHUNK, (c + 1) * CHUNK, TILE):
            (p, q, r), _ = cut(s_ref[at : at + TILE, :], size, 3)
            pq = jnp.concatenate([p, q], axis=1)
            one = one + mm(p, pq, (0, 0))
            two = two + mm(pq, jnp.concatenate([r, q], axis=1), (0, 0))
            three = three + mm(r, r, (0, 0))
        aa, error = two_sum(aa, one[:, :k])
        aa_low = aa_low + error
        ab, error = two_sum(ab, one[:, k:])
        ab_low = ab_low + error
        odd = odd + (two[:k, :k] + two[k:, :k])
        even = even + (two[k:, k:] + three)
    cross, cross_low = two_sum(ab, ab.T)
    total, total_low = two_sum(aa, cross)
    low = ab_low + (odd + 0.5 * even)
    low = (aa_low + (cross_low + total_low)) + (low + low.T)
    high = total + low
    g_ref[0] = packed(high)
    g_ref[1] = packed(low - (high - total))


def local_gram(s):
    rows, k = s.shape
    return pl.pallas_call(
        gram_kernel,
        in_specs=[pl.BlockSpec(memory_space=pl.ANY)],
        out_shape=jax.ShapeDtypeStruct((2, k // 2 + 16, k), F32),
        scratch_shapes=[pltpu.VMEM((rows, k), F32), pltpu.SemaphoreType.DMA((rows // CHUNK,))],
        compiler_params=pltpu.CompilerParams(vmem_limit_bytes=VMEM_LIMIT),
        name="local_gram",
    )(s)


def inverse_factor(a):
    k, n = a.shape[0], 8
    blocks = [a[n * i : n * i + n, :] for i in range(k // n)]
    lane = lax.broadcasted_iota(jnp.int32, (n, k), 1)
    sub = lax.broadcasted_iota(jnp.int32, (n, k), 0)
    full = lambda value: jnp.broadcast_to(value, (n, k))
    column_of = lambda x, j: full(x[:, j : j + 1])
    row_of = lambda x, s: full(x[s : s + 1, :])
    below = [(s, t) for t in range(n) for s in range(t, n)]
    first = [column_of(blocks[0], t) for t in range(n)]
    d = {(s, t): row_of(first[t], s) for s, t in below}
    rows = []
    for p in range(k // n):
        at = n * p
        row = [row_of(blocks[p], s) for s in range(n)]
        done, scale, low = [], [], {}
        for t in range(n):
            scale.append(lax.rsqrt(d[t, t]))
            here = lane == at + t
            done.append(jnp.where(here, scale[t], row[t] * scale[t]))
            for s in range(t + 1, n):
                low[s, t] = d[s, t] * scale[t]
            for u in range(t + 1, n):
                for s in range(u, n):
                    d[s, u] = d[s, u] - low[s, t] * low[u, t]
            for s in range(t + 1, n):
                row[s] = jnp.where(here, 0.0, row[s]) - low[s, t] * done[t]
        out = done[0]
        for t in range(1, n):
            out = jnp.where(sub == t, done[t], out)
        rows.append(out)
        panel = (lane >= at) & (lane < at + n)
        terms = [jnp.where(panel & (lane > at + t), 0.0, done[t]) for t in range(n)]
        for i in range(p + 1, k // n):
            x = blocks[i]
            new = jnp.where(panel, 0.0, x)
            column = []
            for t in range(n):
                c = column_of(x, at + t)
                for u in range(t):
                    c = c - column[u] * low[t, u]
                column.append(c * scale[t])
                new = new - column[t] * terms[t]
            blocks[i] = new
            if i == p + 1:
                ahead = [column_of(x, at + n + s) for s in range(n)]
                parts = [[row_of(c, s) for s in range(n)] for c in column]
                for t in range(n - 1):
                    for s in range(n):
                        ahead[s] = ahead[s] - column[t] * parts[t][s]
                last = parts[n - 1]
                d = {(s, t): row_of(ahead[t], s) - last[s] * last[t] for s, t in below}
    x = jnp.concatenate(rows, axis=0)
    r = lax.broadcasted_iota(jnp.int32, (k, k), 0)
    c = lax.broadcasted_iota(jnp.int32, (k, k), 1)
    return jnp.where(c <= r, x, 0.0)


def mm3(a, b, contract=(1, 0)):
    ah, am = split2(a)
    bh, bm = split2(b)
    return mm(ah, bh, contract) + (mm(ah, bm, contract) + mm(am, bh, contract))


def inverse_factor_near_one(e):
    k = e.shape[0]
    r = lax.broadcasted_iota(jnp.int32, (k, k), 0)
    c = lax.broadcasted_iota(jnp.int32, (k, k), 1)
    half = lambda x: jnp.where(c < r, x, jnp.where(c == r, 0.5 * x, 0.0))
    f = half(e)
    fb = f.astype(BF16)
    ff = mm(fb, fb)
    n = half(mm(fb, fb, (1, 1)) + (ff + ff.T)) - f
    ne = mm3(n, e)
    left = (e + (n + n.T)) + ((ne + ne.T) + mm3(n + ne, n, (1, 1)))
    step = half(left)
    return n - (step + mm(step.astype(BF16), n.astype(BF16)))


def scaled(high, low):
    k = high.shape[0]
    r = lax.broadcasted_iota(jnp.int32, (k, k), 0)
    c = lax.broadcasted_iota(jnp.int32, (k, k), 1)
    diagonal = jnp.where(r == c, high, 0.0)
    row = power_of_two(jnp.sqrt(jnp.max(diagonal, axis=0, keepdims=True)))
    col = power_of_two(jnp.sqrt(jnp.max(diagonal, axis=1, keepdims=True)))
    inv_row, inv_col = 1.0 / row, 1.0 / col
    return (high * inv_row) * inv_col, (low * inv_row) * inv_col, row, inv_row


def by_weight(products, k, n, m):
    block = lambda i, j: products[i * k : (i + 1) * k, j * k : (j + 1) * k]
    return [sum(block(i, t - i) for i in range(n) if 0 <= t - i < m) for t in range(n + m - 1)]


def modes_of(rows, w1, w2):
    k = rows.shape[1]
    h, m, l = split3(rows)
    p = mm(jnp.concatenate([h, m], axis=1), w1)
    q = mm(jnp.concatenate([h, l], axis=1), w2)
    return p[:, :k] + (p[:, k:] + q)


def factors_kernel(count, g_ref, s_ref, chip_ref, up_ref, w1_ref, w2_ref, modes_ref, low_ref, mb_ref, more_ref):
    k = up_ref.shape[0]
    high, low, row, inv_row = scaled(unpacked(g_ref[0]), unpacked(g_ref[1]))
    inv1 = inverse_factor(high)
    size = power_of_two(jnp.max(jnp.abs(inv1), axis=1, keepdims=True))
    p, left = cut(inv1, size, 3)
    inv1 = inv1 - left
    g, left = cut(high, 1.0, 3)
    g += cut(left + low, 2.0**-24, 2)[0]
    p_rows = jnp.concatenate(p, axis=0)
    y, y_low = descending(by_weight(mm(p_rows, jnp.concatenate(g, axis=1)), k, 3, 5))
    size = power_of_two(jnp.max(jnp.abs(y), axis=1, keepdims=True))
    parts, left = cut(y, size, 3)
    parts += cut(left + y_low, size * 2.0**-24, 1)[0]
    gram2, low = descending(by_weight(mm(jnp.concatenate(parts, axis=0), p_rows, (1, 1)), k, 4, 3))
    r = lax.broadcasted_iota(jnp.int32, (k, k), 0)
    c = lax.broadcasted_iota(jnp.int32, (k, k), 1)
    e = jnp.where(c == r, gram2 - 1.0, gram2) + low
    e = 0.5 * (e + e.T)
    near = jnp.sum(e * e) <= 1.0 / 64.0

    @pl.when(near)
    def _():
        more_ref[...] = inverse_factor_near_one(e)

    @pl.when(jnp.logical_not(near))
    def _():
        inv2 = inverse_factor(jnp.where(c == r, 1.0 + e, e))
        more_ref[...] = jnp.where(c == r, inv2 - 1.0, inv2)

    both = jnp.concatenate([inv1, y], axis=1)
    both = both + mm3(more_ref[...], both)
    inverse = (both[:, :k] * inv_row) * math.sqrt(count)
    h, m, l = split3(inverse.T)
    hm = jnp.concatenate([h, m], axis=1)
    w1_ref[...] = jnp.concatenate([hm, hm], axis=0)
    w2_ref[...] = jnp.concatenate([l, h], axis=0)
    up_ref[...] = jnp.where(c >= r, (both[:, k:] * row) * (1.0 / math.sqrt(count)), 0.0)
    for at in (slice(i, i + TILE) for i in range(0, s_ref.shape[0], TILE)):
        modes = modes_of(s_ref[at, :], w1_ref[...], w2_ref[...])
        modes_ref[at, :] = modes
        mb_ref[0, at, :], low_ref[at, :] = split2(modes)
    for at in (slice(i, i + TILE) for i in range(0, s_ref.shape[0], TILE)):
        mb_ref[1, at, :] = modes_of(chip_ref[at, :], w1_ref[...], w2_ref[...]).astype(BF16)


def factors_and_chip_modes(g, s, chip, count):
    rows, k = s.shape
    vmem = pl.BlockSpec(memory_space=pltpu.VMEM)
    return pl.pallas_call(
        lambda *refs: factors_kernel(count, *refs),
        in_specs=[vmem] * 3,
        out_specs=(vmem,) * 6,
        out_shape=(
            jax.ShapeDtypeStruct((k, k), F32),
            pltpu.VMEM((2 * k, 2 * k), BF16),
            pltpu.VMEM((2 * k, k), BF16),
            pltpu.VMEM((rows, k), F32),
            pltpu.VMEM((rows, k), BF16),
            pltpu.VMEM((2, rows, k), BF16),
        ),
        scratch_shapes=[pltpu.VMEM((k, k), F32)],
        compiler_params=pltpu.CompilerParams(vmem_limit_bytes=VMEM_LIMIT),
        name="factors_and_chip_modes",
    )(in_vmem(g), in_vmem(s), in_vmem(chip))


def apply_kernel(
    cols_hbm, modes_ref, low_ref, mb_ref, inner_ref, outer_ref, w1_ref, w2_ref, jb_ref, modes_hbm, jm_ref, red_ref,
    all_ref, cols_ref, sem,
):
    rows, k = low_ref.shape
    block_rows, slots, blk, _ = jb_ref.shape
    place = lax.axis_index("bulk")
    odd = place % 2
    offsets = (rows, (2 - 2 * odd) * rows, 2 * odd * rows)
    at = [pl.ds(pl.multiple_of(offset, blk), rows) for offset in offsets]
    own = pltpu.make_async_copy(mb_ref.at[0], all_ref.at[at[0]], sem.at[0])
    other = pltpu.make_async_copy(mb_ref.at[1], all_ref.at[at[1]], sem.at[1])
    get_cols = pltpu.make_async_copy(cols_hbm, cols_ref, sem.at[2])
    put_modes = pltpu.make_async_copy(modes_ref, modes_hbm, sem.at[3])
    get_cols.start()
    own.start()
    other.start()
    put_modes.start()

    def further(ref):
        for c in range(rows // TILE):
            modes = modes_of(ref[c * TILE : (c + 1) * TILE, :], w1_ref[...], w2_ref[...])
            all_ref[rows_of(c + offsets[2] // TILE, TILE), :] = modes.astype(BF16)

    is_inner = (place % 4 == 1) | (place % 4 == 2)
    pl.when(is_inner)(lambda: further(inner_ref))
    pl.when(jnp.logical_not(is_inner))(lambda: further(outer_ref))
    own.wait()
    other.wait()
    get_cols.wait()
    start = cols_ref[0, 0]

    def apply(r):
        acc = jnp.zeros((blk, k), F32)
        for n in range(0, slots, 2):
            lhs = jnp.concatenate([jb_ref[r, n], jb_ref[r, n + 1]], axis=1)
            picked = []
            for p in (n, n + 1):
                index = cols_ref[r, p] - start + block_rows
                picked.append(all_ref[rows_of(index, blk), :])
            acc = acc + mm(lhs, jnp.concatenate(picked, axis=0))
        jm_ref[rows_of(r, blk), :] = acc.astype(BF16)

    for r in range(block_rows):
        apply(r)

    def project(c, acc):
        at = rows_of(c, TILE)
        return acc + mm(jnp.concatenate([mb_ref[0, at, :], low_ref[at, :]], axis=1), jm_ref[at, :], (0, 0))

    acc = lax.fori_loop(0, rows // TILE, project, jnp.zeros((2 * k, k), F32), unroll=True)
    red_ref[...] = acc[:k, :] + acc[k:, :]
    put_modes.wait()


def apply_and_project(cols, modes, low, mb, inner, outer, w1, w2, jb):
    rows, k = low.shape
    vmem, hbm = pl.BlockSpec(memory_space=pltpu.VMEM), pl.BlockSpec(memory_space=pl.ANY)
    return pl.pallas_call(
        apply_kernel,
        in_specs=[hbm] + [vmem] * 8,
        out_specs=(hbm, vmem, vmem),
        out_shape=(
            jax.ShapeDtypeStruct((rows, k), F32),
            pltpu.VMEM((rows, k), BF16),
            pltpu.VMEM((k, k), F32),
        ),
        scratch_shapes=[
            pltpu.VMEM((3 * rows, k), BF16),
            pltpu.SMEM(cols.shape, jnp.int32),
            pltpu.SemaphoreType.DMA((4,)),
        ],
        compiler_params=pltpu.CompilerParams(vmem_limit_bytes=VMEM_LIMIT),
        name="apply_and_project",
    )(cols, in_vmem(modes), in_vmem(low), in_vmem(mb), in_vmem(inner), in_vmem(outer), in_vmem(w1), in_vmem(w2), in_vmem(jb))


def solution(mesh):
    axes = tuple(mesh.axis_names)
    sizes = dict(mesh.shape)
    n_bulk, n_span = sizes["bulk"], sizes["span"]
    count = n_bulk * n_span
    weight = {"bulk": n_span, "span": 1} if axes[0] == "bulk" else {"bulk": 1, "span": n_bulk}
    bits = lambda n: [1 << i for i in range(n.bit_length() - 1)]
    core_mask = weight["bulk"]
    masks = [m * weight["span"] for m in bits(n_span)] + [m * weight["bulk"] for m in bits(n_bulk)[1:]]
    phases = [masks[i : i + 2] for i in range(0, len(masks), 2)]
    masks_x, masks_y = [core_mask * 2], masks[:1]
    others = [m for m in masks if m not in masks_x + masks_y]
    masks_far = [others[i : i + 2] for i in range(0, len(others), 2)]

    def swap(value, mask):
        return lax.ppermute(value, axes, [(i, i ^ mask) for i in range(count)])

    def exchange(value, phase, add):
        if len(phase) == 1:
            return add(value, swap(value, phase[0]))
        a, b = phase
        pa, pb, pab = swap(value, a), swap(value, b), swap(value, a | b)
        return add(add(value, pa), add(pb, pab))

    def shards(snapshots, jac_blocks, jac_cols):
        rows_total = snapshots.shape[0] * count
        even = lax.axis_index("bulk") % 2 == 0
        pairs = lambda first: [p for i in range(first, n_bulk - 1, 4) for p in ((i, i + 1), (i + 1, i))]
        chip = swap(snapshots, core_mask)
        inner = lax.ppermute(snapshots, "bulk", pairs(1))
        gram = local_gram(snapshots)
        half = gram.shape[1] // 2
        upper, lower = gram[:, :half], gram[:, half:]
        mine = add_pairs(jnp.where(even, upper, lower), swap(jnp.where(even, lower, upper), core_mask))
        mine, chip = lax.optimization_barrier((mine, chip))
        for phase in masks_far:
            mine = exchange(mine, phase, add_pairs)
        mine, inner, late = lax.optimization_barrier((mine, inner, snapshots))
        mine = exchange(mine, masks_x, add_pairs)
        outer = lax.ppermute(late, "bulk", pairs(3))
        along_y, other, across = (swap(mine, mask) for mask in (masks_y[0], core_mask, masks_y[0] | core_mask))
        mine, other = add_pairs(mine, along_y), add_pairs(other, across)
        gram = jnp.concatenate([jnp.where(even, mine, other), jnp.where(even, other, mine)], axis=1)
        factor, w1, w2, modes, low, mb = factors_and_chip_modes(gram, snapshots, chip, rows_total)
        modes, jac_modes, reduced = apply_and_project(jac_cols, modes, low, mb, inner, outer, w1, w2, jac_blocks)
        reduced = reduced + swap(reduced, core_mask)
        for phase in phases:
            reduced = exchange(reduced, phase, jnp.add)
        return modes, factor, jac_modes, reduced / rows_total

    rows = P(("span", "bulk"), None)
    return jax.shard_map(
        shards,
        mesh=mesh,
        in_specs=(rows, P(("span", "bulk"), None, None, None), rows),
        out_specs=(rows, P(), rows, P()),
        check_vma=False,
    )
```

```python
import math

import jax
import jax.numpy as jnp
from jax import lax
from jax.experimental import pallas as pl
from jax.experimental.pallas import tpu as pltpu
from jax.sharding import PartitionSpec as P

F32 = jnp.float32
BF16 = jnp.bfloat16
VMEM_LIMIT = 24 * 1024 * 1024
CHUNK = 512
TILE = 256


def mm(a, b, contract=(1, 0)):
    return lax.dot_general(a, b, (((contract[0],), (contract[1],)), ((), ())), preferred_element_type=F32)


def split2(x):
    h = x.astype(BF16)
    return h, (x - h.astype(F32)).astype(BF16)


def split3(x):
    h = x.astype(BF16)
    r = x - h.astype(F32)
    m = r.astype(BF16)
    return h, m, (r - m.astype(F32)).astype(BF16)


def in_vmem(x):
    return pltpu.with_memory_space_constraint(x, pltpu.VMEM)


def rows_of(i, n):
    return pl.ds(pl.multiple_of(i * n, n), n)


def two_sum(a, b):
    s = a + b
    t = s - a
    return s, (a - (s - t)) + (b - t)


def descending(terms):
    high, low = terms[0], jnp.zeros_like(terms[0])
    for term in terms[1:]:
        high, error = two_sum(high, term)
        low = low + error
    return high, low


def add_pairs(a, b):
    high, error = two_sum(a[0], b[0])
    low = (a[1] + b[1]) + error
    total = high + low
    return jnp.stack([total, low - (total - high)])


def power_of_two(x):
    q = x * float(2**23 + 1)
    return 2.0 * jnp.abs(q - q * (1.0 - 2.0**-24))


def cut(x, size, n):
    grid = size * (1.5 * 2.0**16)
    parts = []
    for _ in range(n):
        part = (x + grid) - grid
        x = x - part
        parts.append(part.astype(BF16))
        grid = grid * 2.0**-8
    return parts, x


def gram_kernel(s_hbm, g_ref, s_ref, sem):
    rows, k = s_ref.shape
    chunks = rows // CHUNK
    copies = [
        pltpu.make_async_copy(s_hbm.at[pl.ds(c * CHUNK, CHUNK)], s_ref.at[pl.ds(c * CHUNK, CHUNK)], sem.at[c])
        for c in range(chunks)
    ]
    for copy in copies:
        copy.start()
    top = jnp.zeros((8, k), F32)
    for c, copy in enumerate(copies):
        copy.wait()
        rows_here = jnp.abs(s_ref[c * CHUNK : (c + 1) * CHUNK, :])
        top = jnp.maximum(top, jnp.max(rows_here.reshape(CHUNK // 8, 8, k), axis=0))
    size = power_of_two(jnp.max(top, axis=0, keepdims=True))
    zero = jnp.zeros((k, k), F32)
    aa, aa_low, ab, ab_low, odd, even = zero, zero, zero, zero, zero, zero
    for c in range(chunks):
        one, two, three = jnp.zeros((k, 2 * k), F32), jnp.zeros((2 * k, 2 * k), F32), zero
        for at in range(c * CHUNK, (c + 1) * CHUNK, TILE):
            (p, q, r), _ = cut(s_ref[at : at + TILE, :], size, 3)
            pq = jnp.concatenate([p, q], axis=1)
            one = one + mm(p, pq, (0, 0))
            two = two + mm(pq, jnp.concatenate([r, q], axis=1), (0, 0))
            three = three + mm(r, r, (0, 0))
        aa, error = two_sum(aa, one[:, :k])
        aa_low = aa_low + error
        ab, error = two_sum(ab, one[:, k:])
        ab_low = ab_low + error
        odd = odd + (two[:k, :k] + two[k:, :k])
        even = even + (two[k:, k:] + three)
    cross, cross_low = two_sum(ab, ab.T)
    total, total_low = two_sum(aa, cross)
    low = ab_low + (odd + 0.5 * even)
    low = (aa_low + (cross_low + total_low)) + (low + low.T)
    high = total + low
    g_ref[0] = high
    g_ref[1] = low - (high - total)


def local_gram(s):
    rows, k = s.shape
    return pl.pallas_call(
        gram_kernel,
        in_specs=[pl.BlockSpec(memory_space=pl.ANY)],
        out_shape=jax.ShapeDtypeStruct((2, k, k), F32),
        scratch_shapes=[pltpu.VMEM((rows, k), F32), pltpu.SemaphoreType.DMA((rows // CHUNK,))],
        compiler_params=pltpu.CompilerParams(vmem_limit_bytes=VMEM_LIMIT),
        name="local_gram",
    )(s)


def inverse_factor(a):
    k, n = a.shape[0], 8
    blocks = [a[n * i : n * i + n, :] for i in range(k // n)]
    lane = lax.broadcasted_iota(jnp.int32, (n, k), 1)
    sub = lax.broadcasted_iota(jnp.int32, (n, k), 0)
    full = lambda value: jnp.broadcast_to(value, (n, k))
    column_of = lambda x, j: full(x[:, j : j + 1])
    row_of = lambda x, s: full(x[s : s + 1, :])
    below = [(s, t) for t in range(n) for s in range(t, n)]
    first = [column_of(blocks[0], t) for t in range(n)]
    d = {(s, t): row_of(first[t], s) for s, t in below}
    rows = []
    for p in range(k // n):
        at = n * p
        row = [row_of(blocks[p], s) for s in range(n)]
        done, scale, low = [], [], {}
        for t in range(n):
            scale.append(lax.rsqrt(d[t, t]))
            here = lane == at + t
            done.append(jnp.where(here, scale[t], row[t] * scale[t]))
            for s in range(t + 1, n):
                low[s, t] = d[s, t] * scale[t]
            for u in range(t + 1, n):
                for s in range(u, n):
                    d[s, u] = d[s, u] - low[s, t] * low[u, t]
            for s in range(t + 1, n):
                row[s] = jnp.where(here, 0.0, row[s]) - low[s, t] * done[t]
        out = done[0]
        for t in range(1, n):
            out = jnp.where(sub == t, done[t], out)
        rows.append(out)
        panel = (lane >= at) & (lane < at + n)
        terms = [jnp.where(panel & (lane > at + t), 0.0, done[t]) for t in range(n)]
        for i in range(p + 1, k // n):
            x = blocks[i]
            new = jnp.where(panel, 0.0, x)
            column = []
            for t in range(n):
                c = column_of(x, at + t)
                for u in range(t):
                    c = c - column[u] * low[t, u]
                column.append(c * scale[t])
                new = new - column[t] * terms[t]
            blocks[i] = new
            if i == p + 1:
                ahead = [column_of(x, at + n + s) for s in range(n)]
                parts = [[row_of(c, s) for s in range(n)] for c in column]
                for t in range(n - 1):
                    for s in range(n):
                        ahead[s] = ahead[s] - column[t] * parts[t][s]
                last = parts[n - 1]
                d = {(s, t): row_of(ahead[t], s) - last[s] * last[t] for s, t in below}
    x = jnp.concatenate(rows, axis=0)
    r = lax.broadcasted_iota(jnp.int32, (k, k), 0)
    c = lax.broadcasted_iota(jnp.int32, (k, k), 1)
    return jnp.where(c <= r, x, 0.0)


def mm3(a, b, contract=(1, 0)):
    ah, am = split2(a)
    bh, bm = split2(b)
    return mm(ah, bh, contract) + (mm(ah, bm, contract) + mm(am, bh, contract))


def inverse_factor_near_one(e):
    k = e.shape[0]
    r = lax.broadcasted_iota(jnp.int32, (k, k), 0)
    c = lax.broadcasted_iota(jnp.int32, (k, k), 1)
    half = lambda x: jnp.where(c < r, x, jnp.where(c == r, 0.5 * x, 0.0))
    f = half(e)
    fb = f.astype(BF16)
    ff = mm(fb, fb)
    n = half(mm(fb, fb, (1, 1)) + (ff + ff.T)) - f
    ne = mm3(n, e)
    left = (e + (n + n.T)) + ((ne + ne.T) + mm3(n + ne, n, (1, 1)))
    step = half(left)
    return n - (step + mm(step.astype(BF16), n.astype(BF16)))


def scaled(high, low):
    k = high.shape[0]
    r = lax.broadcasted_iota(jnp.int32, (k, k), 0)
    c = lax.broadcasted_iota(jnp.int32, (k, k), 1)
    diagonal = jnp.where(r == c, high, 0.0)
    row = power_of_two(jnp.sqrt(jnp.max(diagonal, axis=0, keepdims=True)))
    col = power_of_two(jnp.sqrt(jnp.max(diagonal, axis=1, keepdims=True)))
    inv_row, inv_col = 1.0 / row, 1.0 / col
    return (high * inv_row) * inv_col, (low * inv_row) * inv_col, row, inv_row


def by_weight(products, k, n, m):
    block = lambda i, j: products[i * k : (i + 1) * k, j * k : (j + 1) * k]
    return [sum(block(i, t - i) for i in range(n) if 0 <= t - i < m) for t in range(n + m - 1)]


def modes_of(rows, w1, w2):
    k = rows.shape[1]
    h, m, l = split3(rows)
    p = mm(jnp.concatenate([h, m], axis=1), w1)
    q = mm(jnp.concatenate([h, l], axis=1), w2)
    return p[:, :k] + (p[:, k:] + q)


def factors_kernel(count, g_ref, s_ref, chip_ref, up_ref, w1_ref, w2_ref, modes_ref, low_ref, mb_ref, more_ref):
    k = g_ref.shape[1]
    high, low, row, inv_row = scaled(g_ref[0], g_ref[1])
    inv1 = inverse_factor(high)
    size = power_of_two(jnp.max(jnp.abs(inv1), axis=1, keepdims=True))
    p, left = cut(inv1, size, 3)
    inv1 = inv1 - left
    g, left = cut(high, 1.0, 3)
    g += cut(left + low, 2.0**-24, 2)[0]
    p_rows = jnp.concatenate(p, axis=0)
    y, y_low = descending(by_weight(mm(p_rows, jnp.concatenate(g, axis=1)), k, 3, 5))
    size = power_of_two(jnp.max(jnp.abs(y), axis=1, keepdims=True))
    parts, left = cut(y, size, 3)
    parts += cut(left + y_low, size * 2.0**-24, 1)[0]
    gram2, low = descending(by_weight(mm(jnp.concatenate(parts, axis=0), p_rows, (1, 1)), k, 4, 3))
    r = lax.broadcasted_iota(jnp.int32, (k, k), 0)
    c = lax.broadcasted_iota(jnp.int32, (k, k), 1)
    e = jnp.where(c == r, gram2 - 1.0, gram2) + low
    e = 0.5 * (e + e.T)
    near = jnp.sum(e * e) <= 1.0 / 64.0

    @pl.when(near)
    def _():
        more_ref[...] = inverse_factor_near_one(e)

    @pl.when(jnp.logical_not(near))
    def _():
        inv2 = inverse_factor(jnp.where(c == r, 1.0 + e, e))
        more_ref[...] = jnp.where(c == r, inv2 - 1.0, inv2)

    both = jnp.concatenate([inv1, y], axis=1)
    both = both + mm3(more_ref[...], both)
    inverse = (both[:, :k] * inv_row) * math.sqrt(count)
    h, m, l = split3(inverse.T)
    hm = jnp.concatenate([h, m], axis=1)
    w1_ref[...] = jnp.concatenate([hm, hm], axis=0)
    w2_ref[...] = jnp.concatenate([l, h], axis=0)
    up_ref[...] = jnp.where(c >= r, (both[:, k:] * row) * (1.0 / math.sqrt(count)), 0.0)
    for at in (slice(i, i + TILE) for i in range(0, s_ref.shape[0], TILE)):
        modes = modes_of(s_ref[at, :], w1_ref[...], w2_ref[...])
        modes_ref[at, :] = modes
        mb_ref[0, at, :], low_ref[at, :] = split2(modes)
    for at in (slice(i, i + TILE) for i in range(0, s_ref.shape[0], TILE)):
        mb_ref[1, at, :] = modes_of(chip_ref[at, :], w1_ref[...], w2_ref[...]).astype(BF16)


def factors_and_chip_modes(g, s, chip, count):
    rows, k = s.shape
    vmem = pl.BlockSpec(memory_space=pltpu.VMEM)
    return pl.pallas_call(
        lambda *refs: factors_kernel(count, *refs),
        in_specs=[vmem] * 3,
        out_specs=(vmem,) * 6,
        out_shape=(
            jax.ShapeDtypeStruct((k, k), F32),
            pltpu.VMEM((2 * k, 2 * k), BF16),
            pltpu.VMEM((2 * k, k), BF16),
            pltpu.VMEM((rows, k), F32),
            pltpu.VMEM((rows, k), BF16),
            pltpu.VMEM((2, rows, k), BF16),
        ),
        scratch_shapes=[pltpu.VMEM((k, k), F32)],
        compiler_params=pltpu.CompilerParams(vmem_limit_bytes=VMEM_LIMIT),
        name="factors_and_chip_modes",
    )(in_vmem(g), in_vmem(s), in_vmem(chip))


def apply_kernel(
    cols_hbm, modes_ref, low_ref, mb_ref, inner_ref, outer_ref, w1_ref, w2_ref, jb_ref, modes_hbm, jm_ref, red_ref,
    all_ref, cols_ref, sem,
):
    rows, k = low_ref.shape
    block_rows, slots, blk, _ = jb_ref.shape
    place = lax.axis_index("bulk")
    odd = place % 2
    offsets = (rows, (2 - 2 * odd) * rows, 2 * odd * rows)
    at = [pl.ds(pl.multiple_of(offset, blk), rows) for offset in offsets]
    own = pltpu.make_async_copy(mb_ref.at[0], all_ref.at[at[0]], sem.at[0])
    other = pltpu.make_async_copy(mb_ref.at[1], all_ref.at[at[1]], sem.at[1])
    get_cols = pltpu.make_async_copy(cols_hbm, cols_ref, sem.at[2])
    put_modes = pltpu.make_async_copy(modes_ref, modes_hbm, sem.at[3])
    get_cols.start()
    own.start()
    other.start()
    put_modes.start()

    def further(ref):
        for c in range(rows // TILE):
            modes = modes_of(ref[c * TILE : (c + 1) * TILE, :], w1_ref[...], w2_ref[...])
            all_ref[rows_of(c + offsets[2] // TILE, TILE), :] = modes.astype(BF16)

    is_inner = (place % 4 == 1) | (place % 4 == 2)
    pl.when(is_inner)(lambda: further(inner_ref))
    pl.when(jnp.logical_not(is_inner))(lambda: further(outer_ref))
    own.wait()
    other.wait()
    get_cols.wait()
    start = cols_ref[0, 0]

    def apply(r):
        acc = jnp.zeros((blk, k), F32)
        for n in range(0, slots, 2):
            lhs = jnp.concatenate([jb_ref[r, n], jb_ref[r, n + 1]], axis=1)
            picked = []
            for p in (n, n + 1):
                index = cols_ref[r, p] - start + block_rows
                picked.append(all_ref[rows_of(index, blk), :])
            acc = acc + mm(lhs, jnp.concatenate(picked, axis=0))
        jm_ref[rows_of(r, blk), :] = acc.astype(BF16)

    for r in range(block_rows):
        apply(r)

    def project(c, acc):
        at = rows_of(c, TILE)
        return acc + mm(jnp.concatenate([mb_ref[0, at, :], low_ref[at, :]], axis=1), jm_ref[at, :], (0, 0))

    acc = lax.fori_loop(0, rows // TILE, project, jnp.zeros((2 * k, k), F32), unroll=True)
    red_ref[...] = acc[:k, :] + acc[k:, :]
    put_modes.wait()


def apply_and_project(cols, modes, low, mb, inner, outer, w1, w2, jb):
    rows, k = low.shape
    vmem, hbm = pl.BlockSpec(memory_space=pltpu.VMEM), pl.BlockSpec(memory_space=pl.ANY)
    return pl.pallas_call(
        apply_kernel,
        in_specs=[hbm] + [vmem] * 8,
        out_specs=(hbm, vmem, vmem),
        out_shape=(
            jax.ShapeDtypeStruct((rows, k), F32),
            pltpu.VMEM((rows, k), BF16),
            pltpu.VMEM((k, k), F32),
        ),
        scratch_shapes=[
            pltpu.VMEM((3 * rows, k), BF16),
            pltpu.SMEM(cols.shape, jnp.int32),
            pltpu.SemaphoreType.DMA((4,)),
        ],
        compiler_params=pltpu.CompilerParams(vmem_limit_bytes=VMEM_LIMIT),
        name="apply_and_project",
    )(cols, in_vmem(modes), in_vmem(low), in_vmem(mb), in_vmem(inner), in_vmem(outer), in_vmem(w1), in_vmem(w2), in_vmem(jb))


def solution(mesh):
    axes = tuple(mesh.axis_names)
    sizes = dict(mesh.shape)
    n_bulk, n_span = sizes["bulk"], sizes["span"]
    count = n_bulk * n_span
    weight = {"bulk": n_span, "span": 1} if axes[0] == "bulk" else {"bulk": 1, "span": n_bulk}
    bits = lambda n: [1 << i for i in range(n.bit_length() - 1)]
    core_mask = weight["bulk"]
    masks = [m * weight["span"] for m in bits(n_span)] + [m * weight["bulk"] for m in bits(n_bulk)[1:]]
    phases = [masks[i : i + 2] for i in range(0, len(masks), 2)]
    masks_x, masks_y = [core_mask * 2], masks[:1]
    others = [m for m in masks if m not in masks_x + masks_y]
    masks_far = [others[i : i + 2] for i in range(0, len(others), 2)]

    def swap(value, mask):
        return lax.ppermute(value, axes, [(i, i ^ mask) for i in range(count)])

    def exchange(value, phase, add):
        if len(phase) == 1:
            return add(value, swap(value, phase[0]))
        a, b = phase
        pa, pb, pab = swap(value, a), swap(value, b), swap(value, a | b)
        return add(add(value, pa), add(pb, pab))

    def shards(snapshots, jac_blocks, jac_cols):
        rows_total = snapshots.shape[0] * count
        even = lax.axis_index("bulk") % 2 == 0
        pairs = lambda first: [p for i in range(first, n_bulk - 1, 4) for p in ((i, i + 1), (i + 1, i))]
        inner = lax.ppermute(snapshots, "bulk", pairs(1))
        gram, early = lax.optimization_barrier((local_gram(snapshots), snapshots))
        chip = swap(early, core_mask)
        half = gram.shape[1] // 2
        upper, lower = gram[:, :half], gram[:, half:]
        mine = add_pairs(jnp.where(even, upper, lower), swap(jnp.where(even, lower, upper), core_mask))
        mine, chip = lax.optimization_barrier((mine, chip))
        for phase in masks_far:
            mine = exchange(mine, phase, add_pairs)
        mine, inner, late = lax.optimization_barrier((mine, inner, snapshots))
        mine = exchange(mine, masks_x, add_pairs)
        outer = lax.ppermute(late, "bulk", pairs(3))
        along_y, other, across = (swap(mine, mask) for mask in (masks_y[0], core_mask, masks_y[0] | core_mask))
        mine, other = add_pairs(mine, along_y), add_pairs(other, across)
        gram = jnp.concatenate([jnp.where(even, mine, other), jnp.where(even, other, mine)], axis=1)
        factor, w1, w2, modes, low, mb = factors_and_chip_modes(gram, snapshots, chip, rows_total)
        modes, jac_modes, reduced = apply_and_project(jac_cols, modes, low, mb, inner, outer, w1, w2, jac_blocks)
        reduced = reduced + swap(reduced, core_mask)
        for phase in phases:
            reduced = exchange(reduced, phase, jnp.add)
        return modes, factor, jac_modes, reduced / rows_total

    rows = P(("span", "bulk"), None)
    return jax.shard_map(
        shards,
        mesh=mesh,
        in_specs=(rows, P(("span", "bulk"), None, None, None), rows),
        out_specs=(rows, P(), rows, P()),
        check_vma=False,
    )
```
